512 devices in a mesh: section: 2 (over core), tp: 4 (over x), ep: 64 (over z, y).
Axes of the slice: x: 4, y: 4, z: 16, core: 2. Of those that a mesh axis runs over, the one named last changes fastest.
Arguments:
- tokens: bfloat16 [2, 4096, 2048], P(None, 'ep', 'tp'), may hold values from -12 to 12
- norm_gain: float32 [2, 2048], P('section'), may hold values from 0.1 to 1.9
- expert_gate: bfloat16 [2, 64, 2048, 1024], P('section', 'ep', None, 'tp'), may hold values from -0.125 to 0.125
- expert_up: bfloat16 [2, 64, 2048, 1024], P('section', 'ep', None, 'tp'), may hold values from -0.125 to 0.125
- expert_down: bfloat16 [2, 64, 1024, 2048], P('section', 'ep', 'tp'), may hold values from -0.1875 to 0.1875
- routes: int32 [2, 2, 4096, 8], P('section', None, 'ep'), may hold values from 0 to 63, all different within a row; in each aligned block of 64 rows (0 to 63, 64 to 127, ..., all dimensions but the last counted through in order) at most 9 rows name the same one
- route_weights: float32 [2, 2, 4096, 8], P('section', None, 'ep'), may hold values from 0.1 to 0.4
Outputs:
- layer_states: bfloat16 [2, 2, 4096, 2048], P('section', None, 'ep', 'tp')
The draws below stay inside these ranges and needn't reach their ends.
Inputs may be any that keep to these rules, and one draw needn't show every extreme that they name: `routes`: in each layer and micro-batch, the 64 tokens of one index of ep name one expert at most 9 times, and this is reached; the experts of one token differ.
All inputs are finite; a program needn't handle non-finite values.
Results may differ from the reference program's by a relative error of at most 0.0075.
Values may be sent and summed in bfloat16 or wider, within the bound.
A program may use at most 64 MiB of HBM per device.

```python
import math
import jax
import jax.numpy as jnp
import numpy as np
from jax import lax

D = 2048
FF = 1024
TOK_DEV = 64
MICRO = 2
SECTIONS = 2
EXPERTS = 64
TOPK = 8
CAP = 9
TOKENS = 4096
N_SECTION = 2
N_TP = 4
N_EP = 64


def draw_tokens(key, part):
    key = jax.random.fold_in(key, 11)
    key_base, key_rows, key_cols = jax.random.split(key, 3)
    extent = (MICRO, TOKENS, D)
    incline = 0.45 * 3.0 ** (jnp.arange(D, dtype=jnp.float32) / D)
    columns = incline * jnp.exp(jax.random.uniform(key_cols, (D,), jnp.float32, jnp.log(0.7), jnp.log(1.4)))
    values = jnp.clip(jax.random.normal(key_base, extent, jnp.float32), -3.0, 3.0)
    row_scale = jnp.exp(jax.random.uniform(key_rows, (MICRO, TOKENS, 1), jnp.float32, jnp.log(0.5), jnp.log(2.0)))
    return (values * row_scale * columns).astype(jnp.bfloat16)


def block_scale(own_key, shape, pieces, least, largest):
    level, own = 1.0, jax.random.fold_in(own_key, 6)
    for axis_at, shards_of in pieces:
        heights = jnp.exp(jax.random.uniform(jax.random.fold_in(own, axis_at), (shards_of,), jnp.float32, least / len(pieces), largest / len(pieces)))
        level = level * jnp.repeat(heights, shape[axis_at] // shards_of).reshape([-1 if axis == axis_at else 1 for axis in range(len(shape))])
    return level


def routed_block(key, own, number, rows, amount, top, reach, skew):
    ranking = jax.random.permutation(key, amount)
    heavy_load, common = load_shares(amount, rows * top, reach, skew, True), load_shares(amount, rows * top, reach, skew, False)
    places = jnp.arange(amount)

    def named(tallies, offset_by):
        used = int((tallies > 0).sum())
        fixed = max(1, used // 4)
        passed = fixed + (places - fixed + offset_by * (used - fixed)) % max(1, amount - fixed)
        return jnp.zeros((amount,), jnp.int32).at[ranking[jnp.where(places < fixed, places, passed)]].set(jnp.asarray(tallies, jnp.int32))

    tallies = jnp.where(number % 4 == 0, named(heavy_load, number // 4), named(common, number - number // 4 - 1))
    mixed = jax.random.permutation(jax.random.fold_in(own, 3), amount)
    donor, taker = mixed[0:amount // 2 * 2:2], mixed[1:amount // 2 * 2:2]
    margin = jnp.minimum(tallies[donor] - 1, reach - tallies[taker]) // 2
    margin = jnp.where((donor == ranking[0]) | (taker == ranking[0]) | (tallies[taker] == 0), 0, jnp.maximum(margin, 0))
    passed = jax.random.randint(jax.random.fold_in(own, 4), (amount // 2,), 0, 1 << 20) % (margin + 1)
    tallies = tallies.at[donor].add(-passed).at[taker].add(passed)
    labels = jnp.searchsorted(jnp.cumsum(tallies), jnp.arange(rows * top), side="right").astype(jnp.int32)
    grid = labels.reshape(top, rows).T
    grid = grid[jax.random.permutation(jax.random.fold_in(own, 1), rows)]
    offset_by = jax.random.randint(jax.random.fold_in(own, 2), (rows, 1), 0, top)
    return jnp.take_along_axis(grid, (jnp.arange(top)[None, :] + offset_by) % top, axis=1)


def load_shares(count, total, reach, slope, full):
    weights = [(1 << 20) // math.isqrt(rank ** slope) + 1 for rank in range(1, count + 1)]
    largest = reach if full else min(reach, max(-(-total // count), total * weights[0] // sum(weights)))
    least = 1 if total - largest >= count - 1 else 0
    given, spare = [largest] + [least] * (count - 1), total - largest - least * (count - 1)
    while spare > 0:
        movable = [i for i in range(1, count) if given[i] < largest] or [i for i in range(1, count) if given[i] < reach]
        mass, budget = sum([weights[i] for i in movable]), spare
        for i in movable:
            more = min(reach - given[i], max(1, budget * weights[i] // mass), spare)
            given[i] = given[i] + more
            spare = spare - more
    return np.array(given)


def bell_draw(own_key, shape, deviation, bound, shards=(), held_as=jnp.bfloat16):
    values = jax.random.normal(own_key, shape, jnp.float32) * deviation
    if len(shards) > 0:
        values = block_scale(own_key, shape, shards, -0.22, 0.18) * values
    return jnp.clip(values, min=-bound, max=bound).astype(held_as)


def setup_inputs(seed: int = 0) -> dict:
    seeds = jax.random.split(jax.random.key(seed), 8)
    tokens = draw_tokens(jax.random.fold_in(seeds[7], 71), 0)
    norm_gain = jnp.clip(1.0 + 0.18 * jax.random.normal(seeds[1], (SECTIONS, D), jnp.float32), 0.1, 1.9)
    expert_gate = bell_draw(seeds[2], (SECTIONS, EXPERTS, D, FF), D ** -0.5, 0.125, ((0, 2), (1, 64), (3, 4)))
    expert_up = bell_draw(seeds[3], (SECTIONS, EXPERTS, D, FF), D ** -0.5, 0.125, ((0, 2), (1, 64), (3, 4)))
    expert_down = bell_draw(seeds[4], (SECTIONS, EXPERTS, FF, D), FF ** -0.5, 0.1875, ((0, 2), (1, 64), (2, 4)))
    routes_keys = jax.random.split(jax.random.fold_in(seeds[5], 1), SECTIONS * MICRO * TOKENS // TOK_DEV)
    routes_turns = jax.random.permutation(jax.random.fold_in(seeds[5], 3), SECTIONS * MICRO * TOKENS // TOK_DEV)
    routes = jax.vmap(lambda own, number: routed_block(jax.random.fold_in(seeds[5], 2), own, number, TOK_DEV, EXPERTS, TOPK, CAP, 2))(routes_keys, routes_turns).reshape((SECTIONS, MICRO, TOKENS, TOPK))
    route_weights = jnp.clip(0.1 + 0.3 * jax.random.uniform(seeds[6], (SECTIONS, MICRO, TOKENS, TOPK), jnp.float32) ** block_scale(seeds[6], (SECTIONS, MICRO, TOKENS, TOPK), ((0, 2), (2, 64)), -0.2, 0.2), 0.1, 0.4)
    return dict(tokens=tokens, norm_gain=norm_gain, expert_gate=expert_gate, expert_up=expert_up, expert_down=expert_down, routes=routes, route_weights=route_weights)


EPSILON = 1e-06

def expert_block(operands):
    slot_rows, weight_gate, weight_up, weight_down = operands
    gate_act = jnp.dot(slot_rows, weight_gate, preferred_element_type=jnp.float32)
    up_act = jnp.dot(slot_rows, weight_up, preferred_element_type=jnp.float32)
    hidden = (jax.nn.silu(gate_act) * up_act).astype(jnp.bfloat16)
    group_width = FF // N_TP
    summed = jnp.zeros((slot_rows.shape[0], D), jnp.float32)
    for member in range(N_TP):
        partial_value = jnp.dot(hidden[:, member * group_width:(member + 1) * group_width], weight_down[member * group_width:(member + 1) * group_width], preferred_element_type=jnp.float32).astype(jnp.bfloat16)
        summed = summed + lax.optimization_barrier(partial_value).astype(jnp.float32)
    return summed.astype(jnp.bfloat16)

def apply_layer(inputs, gain_row, weight_gate, weight_up, weight_down, expert_ids, weights):
    values = inputs.astype(jnp.float32)
    mean_square = lax.optimization_barrier(jnp.mean(values * values, axis=1, keepdims=True))
    normed = (values * lax.rsqrt(mean_square + EPSILON) * gain_row).astype(jnp.bfloat16)
    flat_ids = expert_ids.reshape(-1).astype(jnp.int32)
    onehot = (flat_ids[:, None] == jnp.arange(EXPERTS, dtype=jnp.int32)[None, :]).astype(jnp.int32)
    position = lax.optimization_barrier(jnp.sum((jnp.cumsum(onehot, axis=0) - onehot) * onehot, axis=1)).astype(jnp.int32)
    owner_token = jnp.arange(flat_ids.shape[0], dtype=jnp.int32) // TOPK
    buffer = jnp.zeros((EXPERTS, N_EP * CAP, D), jnp.bfloat16).at[flat_ids, position].set(normed[owner_token])
    outputs = lax.map(expert_block, (buffer, weight_gate, weight_up, weight_down))
    picked = outputs[flat_ids, position].reshape(TOKENS, TOPK, D)
    combined = jnp.einsum('tk,tkd->td', weights.astype(jnp.float32), picked.astype(jnp.float32), precision=lax.Precision.HIGHEST)
    return (values + combined).astype(jnp.bfloat16)

def reference(tokens, norm_gain, expert_gate, expert_up, expert_down, routes, route_weights):
    layers = []
    current = [tokens[member] for member in range(MICRO)]
    for layer_index in range(N_SECTION):
        current = [apply_layer(current[member], norm_gain[layer_index], expert_gate[layer_index], expert_up[layer_index], expert_down[layer_index], routes[layer_index, member], route_weights[layer_index, member]) for member in range(MICRO)]
        layers.append(jnp.stack(current))
    return jnp.stack(layers)
```

```python
import jax
import jax.numpy as jnp
from jax import lax
from jax.experimental import pallas as pl
from jax.experimental.pallas import tpu as pltpu
from jax.sharding import PartitionSpec as P

EPSILON = 1e-06
NZ, NY, NX = 16, 4, 4
TOK, TOPK, CAP = 64, 8, 9
D, Q, FFQ = 2048, 512, 256
ROWS = NZ * CAP
MESH = pl.DeviceIdType.MESH
BF, F32 = jnp.bfloat16, jnp.float32


def remote(src, dst, send, recv, device):
    return pltpu.make_async_remote_copy(
        src_ref=src,
        dst_ref=dst,
        send_sem=send,
        recv_sem=recv,
        device_id=device,
        device_id_type=MESH,
    )


def kernel(
    tokens,
    gain_in,
    meta_in,
    gate_in,
    up_in,
    down_in,
    out,
    gate,
    up,
    down,
    gains,
    blocks,
    meta,
    chosen,
    rows,
    parts,
    half,
    half_out,
    half_in,
    done,
    back,
    pick,
    mix,
    ring_out,
    ring_in,
    results,
    sibling_result,
    local_sem,
    pair_send,
    pair_recv,
    zg_send,
    zg_recv,
    zm_send,
    zm_recv,
    yg_send,
    yg_recv,
    yr_send,
    yr_recv,
    xg_send,
    xg_recv,
    xr_send,
    xr_recv,
    zr_send,
    zr_recv,
):
    core = lax.axis_index("section")
    x = lax.axis_index("tp")
    ep = lax.axis_index("ep")
    z, y = ep // NY, ep % NY
    sibling = (1 - core, x, ep)
    z_up = (core, x, ((z + 1) % NZ) * NY + y)
    z_down = (core, x, ((z + NZ - 1) % NZ) * NY + y)

    def at_y(step):
        return (core, x, z * NY + (y + step + NY) % NY)

    x_one = x + 1 - 2 * (x % 2)
    x_three = 3 - x
    x_two = (x + 2) % 4
    quarter = (x, x_one, x_two, x_three)

    def at_x(which):
        return (core, which, ep)

    barrier = pltpu.get_barrier_semaphore()
    friends = [sibling, z_up, z_down, at_y(1), at_y(2), at_y(3), at_x(x_one), at_x(x_three)]
    for friend in friends:
        pl.semaphore_signal(barrier, inc=1, device_id=friend, device_id_type=MESH)
    pl.semaphore_wait(barrier, len(friends))

    def pair_copies():
        sources = (
            (meta_in.at[1 - core], meta.at[0, core]),
            (gain_in, gains.at[core]),
            (gate_in, gate.at[core]),
            (up_in, up.at[core]),
            (down_in, down.at[core]),
        )
        return [
            remote(src, dst, pair_send.at[n], pair_recv.at[n], sibling)
            for n, (src, dst) in enumerate(sources)
        ]

    def own_copies():
        sources = (
            (meta_in.at[core], meta.at[0, core]),
            (gain_in, gains.at[core]),
            (gate_in, gate.at[core]),
            (up_in, up.at[core]),
            (down_in, down.at[core]),
        )
        return [
            pltpu.make_async_copy(src, dst, local_sem.at[n]) for n, (src, dst) in enumerate(sources)
        ]

    pair, own = pair_copies(), own_copies()
    for copy in pair[:1] + own[:1]:
        copy.start()

    def gather_down(layer, step, src):
        return remote(
            blocks.at[layer, src],
            blocks.at[layer, 2 * step - 1],
            zg_send.at[layer, 0, step - 1],
            zg_recv.at[layer, 0, step - 1],
            z_down,
        )

    def gather_up(layer, step, src):
        return remote(
            blocks.at[layer, src],
            blocks.at[layer, 2 * step],
            zg_send.at[layer, 1, step - 1],
            zg_recv.at[layer, 1, step - 1],
            z_up,
        )

    def meta_down(step, src):
        return remote(
            meta.at[src], meta.at[2 * step - 1], zm_send.at[0, step - 1], zm_recv.at[0, step - 1], z_down
        )

    def meta_up(step, src):
        return remote(
            meta.at[src], meta.at[2 * step], zm_send.at[1, step - 1], zm_recv.at[1, step - 1], z_up
        )

    def y_go(layer, n):
        return remote(
            chosen.at[layer, n],
            rows.at[layer, n, 0],
            yg_send.at[layer, n],
            yg_recv.at[layer, n],
            at_y(n),
        )

    def y_back(layer, n):
        return remote(
            done.at[layer, n],
            back.at[layer, n],
            yr_send.at[layer, n],
            yr_recv.at[layer, n],
            at_y(-n),
        )

    def swap(n):
        odd = n % 2
        first, second = 1 + 2 * odd, 3 - 2 * odd
        first_at = x_one + odd * (x_three - x_one)
        second_at = x_three + odd * (x_one - x_three)
        return first, second, at_x(first_at), at_x(second_at)

    def x_gather(layer, n):
        first, second, first_at, second_at = swap(n)
        sems = lambda k: (xg_send.at[layer, n, k], xg_recv.at[layer, n, k])
        own_rows = rows.at[layer, n, 0]
        return (
            remote(own_rows, rows.at[layer, n, first], *sems(0), first_at),
            remote(own_rows, rows.at[layer, n, second], *sems(1), second_at),
            remote(rows.at[layer, n, first], rows.at[layer, n, 2], *sems(2), second_at),
        )

    def x_reduce(layer, n):
        first, second, first_at, second_at = swap(n)
        sems = lambda k: (xr_send.at[layer, n, k], xr_recv.at[layer, n, k])
        return (
            remote(parts.at[layer, n, 2], half.at[layer, n, 1], *sems(0), first_at),
            remote(parts.at[layer, n, first], half.at[layer, n, 0], *sems(1), first_at),
            remote(half_out.at[layer, n], half_in.at[layer, n], *sems(2), second_at),
        )

    def reduce_up(layer, step):
        return remote(
            ring_out.at[layer, 0, step - 1],
            ring_in.at[layer, 0, step - 1],
            zr_send.at[layer, 0, step - 1],
            zr_recv.at[layer, 0, step - 1],
            z_up,
        )

    def reduce_down(layer, step):
        return remote(
            ring_out.at[layer, 1, step - 1],
            ring_in.at[layer, 1, step - 1],
            zr_send.at[layer, 1, step - 1],
            zr_recv.at[layer, 1, step - 1],
            z_down,
        )

    def build_selection(layer):
        lane = lax.broadcasted_iota(jnp.int32, (TOPK, 128), 1)
        low = lane < TOK
        a = lax.broadcasted_iota(jnp.int32, (128, 128), 0)
        b = lax.broadcasted_iota(jnp.int32, (128, 128), 1)
        before = jnp.where((a < b) & ((a < TOK) == (b < TOK)), 1.0, 0.0).astype(BF)
        row_number = lax.broadcasted_iota(jnp.int32, (ROWS, 128), 0).astype(F32)
        high_one = jnp.where(lax.broadcasted_iota(jnp.int32, (1, 128), 1) < TOK, 0.0, 1.0)
        experts = [(z * NY + (y + n) % NY).astype(F32) for n in range(NY)]

        def pair_of_blocks(q, carry):
            named = jnp.where(low, meta[2 * q, layer, 0:TOPK], meta[2 * q + 1, layer, 0:TOPK])
            weight = jnp.where(
                low, meta[2 * q, layer, TOPK : 2 * TOPK], meta[2 * q + 1, layer, TOPK : 2 * TOPK]
            )
            base = (2 * q).astype(F32) + high_one
            lanes = pl.ds(pl.multiple_of(q * 128, 128), 128)
            for n in range(NY):
                same = jnp.where(named == experts[n], 1.0, 0.0)
                count = jnp.dot(same.astype(BF), before, preferred_element_type=F32)
                position = jnp.sum(count, axis=0, keepdims=True)
                hits = jnp.sum(same, axis=0, keepdims=True)
                share = jnp.sum(same * weight, axis=0, keepdims=True)
                slot = jnp.where(hits > 0.5, position + CAP * base, -1.0)
                hit = row_number == slot
                pick[n, :, lanes] = jnp.where(hit, 1.0, 0.0).astype(BF)
                mix[q, n * ROWS : (n + 1) * ROWS, :] = jnp.where(hit, share, 0.0).astype(BF)
            return carry

        lax.fori_loop(0, NZ // 2, pair_of_blocks, 0)

    def expert(layer, n):
        first, second, _, _ = swap(n)
        total = jnp.zeros((ROWS, 1), F32)
        for s in range(4):
            value = rows[layer, n, s].astype(F32)
            total = total + jnp.sum(value * value, axis=1, keepdims=True)
        scale = lax.rsqrt(total / D + EPSILON)
        gate_act = jnp.zeros((ROWS, FFQ), F32)
        up_act = jnp.zeros((ROWS, FFQ), F32)
        for s in range(4):
            span = pl.ds(pl.multiple_of(quarter[s] * Q, Q), Q)
            value = rows[layer, n, s].astype(F32)
            normed = (value * scale * gains[layer, 0:1, span]).astype(BF)
            gate_act += jnp.dot(normed, gate[layer, span, :], preferred_element_type=F32)
            up_act += jnp.dot(normed, up[layer, span, :], preferred_element_type=F32)
        hidden = (gate_act / (1.0 + jnp.exp(-gate_act)) * up_act).astype(BF)
        sends = x_reduce(layer, n)
        for s in (2, 1, 3, 0):
            span = pl.ds(pl.multiple_of(quarter[s] * Q, Q), Q)
            parts[layer, n, s] = jnp.dot(
                hidden, down[layer, :, span], preferred_element_type=F32
            ).astype(BF)
            if s == 2:
                sends[0].start()
            if s == 3:
                sends[1].start()

    def mixed(layer, q):
        returned = back[layer].reshape(NY * ROWS, Q)
        return lax.dot_general(
            mix[q], returned, (((0,), (0,)), ((), ())), preferred_element_type=F32
        )

    def one_layer(layer, carry):
        gather_down(layer, 1, 0).start()
        gather_up(layer, 1, 0).start()

        @pl.when(layer == 0)
        def _():
            for copy in pair[1:] + own[1:]:
                copy.start()
            own[0].wait()
            pair[0].wait()
            meta_down(1, 0).start()
            meta_up(1, 0).start()

        def gather_step(step, c):
            gather_down(layer, step - 1, 0).wait_recv()
            gather_down(layer, step, 2 * step - 3).start()
            gather_up(layer, step - 1, 0).wait_recv()

            @pl.when(step < 8)
            def _():
                gather_up(layer, step, 2 * step - 2).start()

            @pl.when(layer == 0)
            def _():
                meta_down(step - 1, 0).wait_recv()
                meta_down(step, 2 * step - 3).start()
                meta_up(step - 1, 0).wait_recv()

                @pl.when(step < 8)
                def _():
                    meta_up(step, 2 * step - 2).start()

            return c

        lax.fori_loop(2, 9, gather_step, 0)
        gather_down(layer, 8, 0).wait_recv()

        @pl.when(layer == 0)
        def _():
            meta_down(8, 0).wait_recv()

        build_selection(layer)
        everything = blocks[layer].reshape(NZ * TOK, Q)
        for n in (1, 2, 3, 0):
            value = jnp.dot(pick[n], everything, preferred_element_type=F32).astype(BF)
            if n == 0:
                rows[layer, 0, 0] = value
            else:
                chosen[layer, n] = value
                y_go(layer, n).start()

        @pl.when(layer == 0)
        def _():
            for copy in pair[1:] + own[1:]:
                copy.wait()

        def tick(t, c):
            @pl.when(t < 4)
            def _():
                @pl.when(t > 0)
                def _():
                    y_go(layer, t).wait_recv()

                own_first, own_second, _ = x_gather(layer, t)
                own_first.start()
                own_second.start()

            @pl.when((t >= 1) & (t < 5))
            def _():
                got_first, _, forward = x_gather(layer, t - 1)
                got_first.wait_recv()
                forward.start()

            @pl.when((t >= 3) & (t < 7))
            def _():
                n = t - 3
                far, near, onward = x_reduce(layer, n)
                far.wait_recv()
                _, second, _, _ = swap(n)
                half_out[layer, n] = (
                    parts[layer, n, second].astype(F32) + half[layer, n, 1].astype(F32)
                ).astype(BF)
                onward.start()

            @pl.when((t >= 2) & (t < 6))
            def _():
                _, got_second, forward = x_gather(layer, t - 2)
                got_second.wait_recv()
                forward.wait_recv()
                expert(layer, t - 2)

            @pl.when(t >= 4)
            def _():
                n = t - 4
                far, near, onward = x_reduce(layer, n)
                near.wait_recv()
                onward.wait_recv()
                value = (
                    parts[layer, n, 0].astype(F32)
                    + half[layer, n, 0].astype(F32)
                    + half_in[layer, n].astype(F32)
                ).astype(BF)

                @pl.when(n == 0)
                def _():
                    back[layer, 0] = value

                @pl.when(n > 0)
                def _():
                    done[layer, n] = value
                    y_back(layer, n).start()

            return c

        lax.fori_loop(0, 8, tick, 0)
        for n in range(1, 4):
            y_back(layer, n).wait_recv()

        value = mixed(layer, NZ // 2 - 1)
        ring_out[layer, 0, 0] = value[TOK:].astype(BF)
        reduce_up(layer, 1).start()
        ring_out[layer, 1, 0] = value[:TOK].astype(BF)
        reduce_down(layer, 1).start()

        def reduce_step(step, c):
            value = mixed(layer, NZ // 2 - step)
            reduce_up(layer, step - 1).wait_recv()
            ring_out[layer, 0, step - 1] = (
                value[TOK:] + ring_in[layer, 0, step - 2].astype(F32)
            ).astype(BF)
            reduce_up(layer, step).start()
            reduce_down(layer, step - 1).wait_recv()
            ring_out[layer, 1, step - 1] = (
                value[:TOK] + ring_in[layer, 1, step - 2].astype(F32)
            ).astype(BF)
            reduce_down(layer, step).start()
            return c

        lax.fori_loop(2, 8, reduce_step, 0)
        value = mixed(layer, 0)
        reduce_up(layer, 7).wait_recv()
        ring_out[layer, 0, 7] = (value[TOK:] + ring_in[layer, 0, 6].astype(F32)).astype(BF)
        reduce_up(layer, 8).start()
        reduce_down(layer, 7).wait_recv()
        mine = value[:TOK] + blocks[layer, 0].astype(F32) + ring_in[layer, 1, 6].astype(F32)
        reduce_up(layer, 8).wait_recv()
        final = (mine + ring_in[layer, 0, 7].astype(F32)).astype(BF)
        results[layer] = final

        @pl.when(layer == 0)
        def _():
            blocks[1, 0] = final

        return carry

    blocks[0, 0] = tokens[core]
    lax.fori_loop(0, 2, one_layer, 0)
    last = remote(results.at[1 - core], sibling_result, pair_send.at[5], pair_recv.at[5], sibling)
    last.start()
    out[core] = results[core]

    def drain(layer, carry):
        def ring(step, c):
            gather_down(layer, step, 0).wait_send()
            reduce_up(layer, step).wait_send()

            @pl.when(step < 8)
            def _():
                gather_up(layer, step, 0).wait_send()
                reduce_down(layer, step).wait_send()

            @pl.when(layer == 0)
            def _():
                meta_down(step, 0).wait_send()

                @pl.when(step < 8)
                def _():
                    meta_up(step, 0).wait_send()

            return c

        lax.fori_loop(1, 9, ring, 0)

        def chunk(n, c):
            for copy in x_gather(layer, n) + x_reduce(layer, n):
                copy.wait_send()

            @pl.when(n > 0)
            def _():
                y_go(layer, n).wait_send()
                y_back(layer, n).wait_send()

            return c

        lax.fori_loop(0, 4, chunk, 0)
        return carry

    lax.fori_loop(0, 2, drain, 0)
    last.wait()
    out[1 - core] = sibling_result[...]


def shards(tokens, norm_gain, expert_gate, expert_up, expert_down, routes, route_weights):
    named = jnp.swapaxes(routes[0], 1, 2).astype(F32)
    weight = jnp.swapaxes(route_weights[0], 1, 2)
    meta = jnp.concatenate([named, weight], axis=1)
    meta = jnp.concatenate([meta, meta], axis=2)
    gain = jnp.broadcast_to(norm_gain, (8, D))
    vmem = pl.BlockSpec(memory_space=pltpu.VMEM)
    anywhere = pl.BlockSpec(memory_space=pl.ANY)
    dma = pltpu.SemaphoreType.DMA
    out = pl.pallas_call(
        kernel,
        out_shape=jax.ShapeDtypeStruct((2, TOK, Q), BF),
        in_specs=[vmem, vmem, vmem, anywhere, anywhere, anywhere],
        out_specs=vmem,
        scratch_shapes=[
            pltpu.VMEM((2, D, FFQ), BF),
            pltpu.VMEM((2, D, FFQ), BF),
            pltpu.VMEM((2, FFQ, D), BF),
            pltpu.VMEM((2, 8, D), F32),
            pltpu.VMEM((2, NZ, TOK, Q), BF),
            pltpu.VMEM((NZ, 2, 2 * TOPK, 128), F32),
            pltpu.VMEM((2, NY, ROWS, Q), BF),
            pltpu.VMEM((2, NY, 4, ROWS, Q), BF),
            pltpu.VMEM((2, NY, 4, ROWS, Q), BF),
            pltpu.VMEM((2, NY, 2, ROWS, Q), BF),
            pltpu.VMEM((2, NY, ROWS, Q), BF),
            pltpu.VMEM((2, NY, ROWS, Q), BF),
            pltpu.VMEM((2, NY, ROWS, Q), BF),
            pltpu.VMEM((2, NY, ROWS, Q), BF),
            pltpu.VMEM((NY, ROWS, NZ * TOK), BF),
            pltpu.VMEM((NZ // 2, NY * ROWS, 128), BF),
            pltpu.VMEM((2, 2, 8, TOK, Q), BF),
            pltpu.VMEM((2, 2, 8, TOK, Q), BF),
            pltpu.VMEM((2, TOK, Q), BF),
            pltpu.VMEM((TOK, Q), BF),
            dma((5,)),
            dma((6,)),
            dma((6,)),
            dma((2, 2, 8)),
            dma((2, 2, 8)),
            dma((2, 8)),
            dma((2, 8)),
            dma((2, 4)),
            dma((2, 4)),
            dma((2, 4)),
            dma((2, 4)),
            dma((2, 4, 3)),
            dma((2, 4, 3)),
            dma((2, 4, 3)),
            dma((2, 4, 3)),
            dma((2, 2, 8)),
            dma((2, 2, 8)),
        ],
        compiler_params=pltpu.CompilerParams(
            collective_id=0, has_side_effects=True, vmem_limit_bytes=56 * 1024 * 1024
        ),
        cost_estimate=pl.CostEstimate(
            flops=2 * 2 * 576 * D * 768, bytes_accessed=8 * 1024 * 1024, transcendentals=0
        ),
    )(tokens, gain, meta, expert_gate[0, 0], expert_up[0, 0], expert_down[0, 0])
    return out[None]


def solution(mesh):
    placed = (
        P(None, "ep", "tp"),
        P("section", None),
        P("section", "ep", None, "tp"),
        P("section", "ep", None, "tp"),
        P("section", "ep", "tp", None),
        P("section", None, "ep", None),
        P("section", None, "ep", None),
    )
    return jax.shard_map(
        shards,
        mesh=mesh,
        in_specs=placed,
        out_specs=P("section", None, "ep", "tp"),
        check_vma=False,
    )
```

```python
import jax
import jax.numpy as jnp
from jax import lax
from jax.experimental import pallas as pl
from jax.experimental.pallas import tpu as pltpu
from jax.sharding import PartitionSpec as P

EPSILON = 1e-06
NZ, NY, NX = 16, 4, 4
TOK, TOPK, CAP = 64, 8, 9
D, Q, FFQ = 2048, 512, 256
ROWS = NZ * CAP
MESH = pl.DeviceIdType.MESH
PLACE = (0, 1, 15, 2, 14, 3, 13, 4, 12, 6, 10, 5, 11, 7, 9, 8)
AT = {distance: p for p, distance in enumerate(PLACE)}
PARENT = {
    3: (0, -3), 13: (0, 3), 2: (0, -2), 14: (0, 2), 1: (0, -1), 15: (0, 1),
    6: (3, -3), 4: (3, -1), 5: (3, -2), 10: (13, 3), 12: (13, 1),
    7: (6, -1), 8: (10, 2), 9: (10, 1), 11: (10, -1),
}
CHILDREN = {
    root: [child for child, (parent, _) in PARENT.items() if parent == root]
    for root in (0, 3, 13, 6, 10)
}
GROUPS = 3
PART = ROWS // GROUPS
PAIRS = tuple(range(g * PART // (2 * CAP), -(-(g + 1) * PART // (2 * CAP))) for g in range(GROUPS))
MIXES = tuple((q, g) for g in range(GROUPS) for q in PAIRS[g])
TURN = (0, 1, 3, 2)
WIDE = NY * PART
HALF = WIDE // 2
DIRECT = (False, False, False)
BF, F32 = jnp.bfloat16, jnp.float32

SCHEDULE = (
    "z 0", "z 13", "z 3", "zw 2", "zw 1", "zw 14", "zw 15", "b 2", "b 1", "b 0", "s 0", "w",
    "z 10", "xs 0 0", "z 6", "xs 0 1", "zw 4", "zw 12", "zw 5", "b 3", "b 5", "b 4", "s 1",
    "zw 11", "zw 8", "zw 9", "b 7", "zw 7", "b 6", "xp 0 0", "s 2", "xp 0 1", "xs 1 0",
    "xs 1 1", "xs 2 0", "xs 2 1", "e 0 1", "xp 1 1", "xp 2 0", "xp 1 0", "xp 2 1", "turn", "e 0 0",
    "f 0 1", "e 2 1", "e 2 0", "f 0 0", "e 1 1", "f 2 1", "e 1 0", "d 0 0", "f 2 0",
    "d 0 1", "f 1 1", "d 2 1", "f 1 0", "d 2 0", "r 0", "d 1 1", "c 1", "d 1 0", "r 2",
    "c 7", "c 6", "r 1", "c 3", "c 5", "c 4", "p 10", "p 6", "c 2", "c 0", "p 13", "p 3",
    "settle", "bn", "last",
)


def remote(src, dst, send, recv, device):
    return pltpu.make_async_remote_copy(
        src_ref=src,
        dst_ref=dst,
        send_sem=send,
        recv_sem=recv,
        device_id=device,
        device_id_type=MESH,
    )


def kernel(
    tokens,
    gain_in,
    named_in,
    weight_in,
    gate_in,
    up_in,
    down_in,
    out,
    gate,
    up,
    down,
    gains,
    blocks,
    named,
    weight,
    own_meta,
    meta,
    chosen,
    rows,
    parts,
    half,
    half_out,
    done,
    back,
    pick,
    mix,
    ring_out,
    ring_in,
    results,
    local_sem,
    pair_send,
    pair_recv,
    zg_send,
    zg_recv,
    zm_send,
    zm_recv,
    yg_send,
    yg_recv,
    yr_send,
    yr_recv,
    xg_send,
    xg_recv,
    xr_send,
    xr_recv,
    zr_send,
    zr_recv,
    turn,
):
    core = lax.axis_index("section")
    x = lax.axis_index("tp")
    ep = lax.axis_index("ep")
    z, y = ep // NY, ep % NY
    sibling = (1 - core, x, ep)

    def at_z(step):
        return (core, x, ((z + step + NZ) % NZ) * NY + y)

    def at_y(step):
        return (core, x, z * NY + (y + step + NY) % NY)

    x_one = x + 1 - 2 * (x % 2)
    x_three = 3 - x
    x_two = (x + 2) % 4
    quarter = (x, x_one, x_two, x_three)

    def at_x(which):
        return (core, which, ep)

    def pair_copies():
        sources = (
            (own_meta.at[1 - core], meta.at[0, core]),
            (gain_in, gains.at[core]),
            (gate_in, gate.at[core]),
            (up_in, up.at[core]),
            (down_in, down.at[core]),
        )
        return [
            remote(src, dst, pair_send.at[n], pair_recv.at[n], sibling)
            for n, (src, dst) in enumerate(sources)
        ]

    def own_copies():
        sources = (
            (tokens.at[core], blocks.at[0, 0]),
            (named_in, named),
            (weight_in, weight),
            (gain_in, gains.at[core]),
            (gate_in, gate.at[core]),
            (up_in, up.at[core]),
            (down_in, down.at[core]),
        )
        return [
            pltpu.make_async_copy(src, dst, local_sem.at[n]) for n, (src, dst) in enumerate(sources)
        ]

    pair, own = pair_copies(), own_copies()
    for copy in own:
        copy.start()

    barrier = pltpu.get_barrier_semaphore()
    friends = [sibling, at_y(1), at_y(2), at_y(3), at_x(x_one), at_x(x_three)]
    if any(DIRECT):
        friends += [at_x(x_two)]
    friends += [at_z(step) for step in (-3, -2, -1, 1, 2, 3)]
    for friend in friends:
        pl.semaphore_signal(barrier, inc=1, device_id=friend, device_id_type=MESH)
    own[1].wait()
    own[2].wait()
    for micro in range(2):
        entry = jnp.concatenate([named[micro].astype(F32), weight[micro]], axis=0)
        own_meta[micro] = jnp.concatenate([entry, entry], axis=1).astype(BF)
    meta[0, core] = own_meta[core]
    own[0].wait()
    pl.semaphore_wait(barrier, len(friends))

    for copy in pair:
        copy.start()

    def gather(layer, distance):
        parent, step = PARENT[distance]
        p = AT[distance]
        return remote(
            blocks.at[layer, AT[parent]],
            blocks.at[layer, p],
            zg_send.at[layer, p],
            zg_recv.at[layer, p],
            at_z(step),
        )

    def gather_meta(distance):
        parent, step = PARENT[distance]
        p = AT[distance]
        return remote(meta.at[AT[parent]], meta.at[p], zm_send.at[p], zm_recv.at[p], at_z(step))

    def reduce(layer, distance):
        _, step = PARENT[distance]
        p = AT[distance]
        return remote(
            ring_out.at[layer, p],
            ring_in.at[layer, p],
            zr_send.at[layer, p],
            zr_recv.at[layer, p],
            at_z(-step),
        )

    def y_go(layer, g, k):
        return remote(
            chosen.at[layer, g, pl.ds(k * PART, PART)],
            rows.at[layer, g, 0, pl.ds(k * PART, PART)],
            yg_send.at[layer, g, k],
            yg_recv.at[layer, g, k],
            at_y(TURN[k]),
        )

    def y_back(layer, g, k):
        return remote(
            done.at[layer, g, pl.ds(k * PART, PART)],
            back.at[layer, g, pl.ds(k * PART, PART)],
            yr_send.at[layer, g, k],
            yr_recv.at[layer, g, k],
            at_y(-TURN[k]),
        )

    def x_gather(layer, g, h):
        first, second = (1, 3) if h == 0 else (3, 1)
        span = pl.ds(h * HALF, HALF)
        source = 0 if DIRECT[g] else first
        far = 2 if DIRECT[g] else second
        return [
            remote(
                rows.at[layer, g, src, span],
                rows.at[layer, g, dst, span],
                xg_send.at[layer, g, h, n],
                xg_recv.at[layer, g, h, n],
                at_x(quarter[to]),
            )
            for n, (src, dst, to) in enumerate(
                ((0, first, first), (0, second, second), (source, 2, far))
            )
        ]

    def x_reduce(layer, g, h):
        first, second = (1, 3) if h == 0 else (3, 1)
        span = pl.ds(h * HALF, HALF)
        if DIRECT[g]:
            ways = [(parts.at[layer, g, n, span], n) for n in (2, 1, 3)]
        else:
            ways = [
                (parts.at[layer, g, 2, span], first),
                (parts.at[layer, g, first, span], first),
                (half_out.at[layer, g, span], second),
            ]
        return [
            remote(
                src,
                half.at[layer, g, n, span],
                xr_send.at[layer, g, h, n],
                xr_recv.at[layer, g, h, n],
                at_x(quarter[to]),
            )
            for n, (src, to) in enumerate(ways)
        ]

    def build_selection(layer, pairs):
        lane = lax.broadcasted_iota(jnp.int32, (2 * TOPK, 128), 1)
        low = lane < TOK
        a = lax.broadcasted_iota(jnp.int32, (128, 128), 0)
        b = lax.broadcasted_iota(jnp.int32, (128, 128), 1)
        before = jnp.where((a < b) & ((a < TOK) == (b < TOK)), 1.0, 0.0).astype(BF)
        row_number = lax.broadcasted_iota(jnp.int32, (PART, 128), 0).astype(F32)
        high_one = jnp.where(lax.broadcasted_iota(jnp.int32, (1, 128), 1) < TOK, 0.0, 1.0)
        for q in pairs:
            entry = jnp.where(
                low, meta[2 * q, layer].astype(F32), meta[2 * q + 1, layer].astype(F32)
            )
            named, weight = entry[:TOPK], entry[TOPK:]
            same = [
                jnp.where(named == (z * NY + (y + TURN[k]) % NY).astype(F32), 1.0, 0.0)
                for k in range(NY)
            ]
            count = jnp.dot(
                jnp.concatenate(same, axis=0).astype(BF), before, preferred_element_type=F32
            )
            for k in range(NY):
                position = jnp.sum(count[k * TOPK : (k + 1) * TOPK], axis=0, keepdims=True)
                hits = jnp.sum(same[k], axis=0, keepdims=True)
                share = jnp.sum(same[k] * weight, axis=0, keepdims=True)
                slot = jnp.where(hits > 0.5, position + CAP * (2 * q + high_one), -1.0)
                for m, (other, g) in enumerate(MIXES):
                    if other == q:
                        hit = row_number + g * PART == slot
                        at = (q - PAIRS[g][0]) * 128
                        pick[layer, g, k * PART : (k + 1) * PART, at : at + 128] = jnp.where(
                            hit, 1.0, 0.0
                        ).astype(BF)
                        mix[layer, m, k * PART : (k + 1) * PART, :] = jnp.where(
                            hit, share, 0.0
                        ).astype(BF)

    def expert(layer, g, h):
        span_rows = slice(h * HALF, (h + 1) * HALF)
        total = jnp.zeros((HALF, 1), F32)
        for s in range(4):
            value = rows[layer, g, s, span_rows].astype(F32)
            total = total + jnp.sum(value * value, axis=1, keepdims=True)
        scale = lax.rsqrt(total / D + EPSILON)
        gate_act = jnp.zeros((HALF, FFQ), F32)
        up_act = jnp.zeros((HALF, FFQ), F32)
        for s in range(4):
            span = pl.ds(pl.multiple_of(quarter[s] * Q, Q), Q)
            value = rows[layer, g, s, span_rows].astype(F32)
            normed = (value * scale * gains[layer, 0:1, span]).astype(BF)
            gate_act += jnp.dot(normed, gate[layer, span, :], preferred_element_type=F32)
            up_act += jnp.dot(normed, up[layer, span, :], preferred_element_type=F32)
        hidden = (gate_act / (1.0 + jnp.exp(-gate_act)) * up_act).astype(BF)
        sends = x_reduce(layer, g, h)
        first = 1 if h == 0 else 3
        order = (2, 1, 3, 0) if DIRECT[g] else (2, first, 4 - first, 0)
        for n, s in enumerate(order):
            span = pl.ds(pl.multiple_of(quarter[s] * Q, Q), Q)
            parts[layer, g, s, span_rows] = jnp.dot(
                hidden, down[layer, :, span], preferred_element_type=F32
            ).astype(BF)
            if n < (3 if DIRECT[g] else 2):
                sends[n].start()

    def one_layer(layer, carry):
        sums = {}

        def first_only(action):
            pl.when(layer == 0)(action)

        def z_pass(root):
            if root:
                gather(layer, root).wait_recv()
            for distance in CHILDREN[root]:
                gather(layer, distance).start()

            @first_only
            def _():
                if root:
                    gather_meta(root).wait_recv()
                else:
                    pair[0].wait()
                for distance in CHILDREN[root]:
                    gather_meta(distance).start()

        def z_wait(*distances):
            for distance in distances:
                gather(layer, distance).wait_recv()

            @first_only
            def _():
                for distance in distances:
                    gather_meta(distance).wait_recv()

        def build(*pairs):
            first_only(lambda: build_selection(0, pairs))

        def build_next():
            first_only(lambda: build_selection(1, range(NZ // 2)))

        def select(g):
            pairs = PAIRS[g]
            source = blocks[layer, 2 * pairs[0] : 2 * pairs[-1] + 2].reshape(-1, Q)
            value = jnp.dot(
                pick[layer, g, :, 0 : len(pairs) * 128], source, preferred_element_type=F32
            ).astype(BF)
            chosen[layer, g] = value
            for k in (1, 2, 3):
                y_go(layer, g, k).start()
            rows[layer, g, 0, 0:PART] = value[:PART]

        def x_send(g, h):
            for k in (2 * h, 2 * h + 1):
                if k:
                    y_go(layer, g, k).wait_recv()
            copies = x_gather(layer, g, h)
            for copy in copies if DIRECT[g] else copies[:2]:
                copy.start()

        def x_pass(g, h):
            copies = x_gather(layer, g, h)
            copies[0].wait_recv()
            if not DIRECT[g]:
                copies[2].start()

        def weights():
            @first_only
            def _():
                for copy in pair[1:] + own[3:]:
                    copy.wait()

        def work(g, h):
            copies = x_gather(layer, g, h)
            copies[1].wait_recv()
            copies[2].wait_recv()
            expert(layer, g, h)

        def fold(g, h):
            if not DIRECT[g]:
                span = slice(h * HALF, (h + 1) * HALF)
                copies = x_reduce(layer, g, h)
                copies[0].wait_recv()
                half_out[layer, g, span] = (
                    parts[layer, g, 3 - 2 * h, span].astype(F32)
                    + half[layer, g, 0, span].astype(F32)
                ).astype(BF)
                copies[2].start()

        def finish(g, h):
            span = slice(h * HALF, (h + 1) * HALF)
            copies = x_reduce(layer, g, h)
            terms = (0, 1, 2) if DIRECT[g] else (1, 2)
            for n in terms:
                copies[n].wait_recv()
            value = parts[layer, g, 0, span].astype(F32)
            for n in terms:
                value = value + half[layer, g, n, span].astype(F32)
            value = value.astype(BF)
            done[layer, g, span] = value
            for k in (2 * h, 2 * h + 1):
                if k:
                    y_back(layer, g, k).start()
            if h == 0:
                back[layer, g, 0:PART] = value[:PART]

        def returned(g):
            for k in (1, 2, 3):
                y_back(layer, g, k).wait_recv()

        def collect(distance, value):
            for child in CHILDREN.get(distance, ()):
                reduce(layer, child).wait_recv()
                value = value + ring_in[layer, AT[child]].astype(F32)
            return value

        def pass_on(distance):
            ring_out[layer, AT[distance]] = collect(distance, sums[distance]).astype(BF)
            reduce(layer, distance).start()

        def combine(q):
            value = None
            for m, (other, g) in enumerate(MIXES):
                if other == q:
                    term = lax.dot_general(
                        mix[layer, m],
                        back[layer, g],
                        (((0,), (0,)), ((), ())),
                        preferred_element_type=F32,
                    )
                    value = term if value is None else value + term
            for k in range(2):
                distance = PLACE[2 * q + k]
                sums[distance] = value[k * TOK : (k + 1) * TOK]
                if distance not in CHILDREN:
                    pass_on(distance)

        def settle():
            for distance in PLACE[1:]:
                gather(layer, distance).wait_send()
                if distance not in (3, 13):
                    reduce(layer, distance).wait_send()

            @first_only
            def _():
                for distance in PLACE[1:]:
                    gather_meta(distance).wait_send()

            for g in range(GROUPS):
                for k in (1, 2, 3):
                    y_go(layer, g, k).wait_send()
                    y_back(layer, g, k).wait_send()
                for h in range(2):
                    for copy in x_gather(layer, g, h) + x_reduce(layer, g, h):
                        copy.wait_send()

        def last():
            for distance in (3, 13):
                reduce(layer, distance).wait_send()
            final = collect(0, sums[0] + blocks[layer, 0].astype(F32)).astype(BF)
            results[layer] = final

            @first_only
            def _():
                blocks[1, 0] = final

        steps = dict(
            z=z_pass, zw=z_wait, b=build, bn=build_next, s=select, xs=x_send, xp=x_pass,
            w=weights, e=work, f=fold, d=finish, r=returned, c=combine, p=pass_on,
            settle=settle, last=last,
        )
        @pl.when((layer == 0) & (core == 1))
        def _():
            pl.semaphore_wait(turn, 1)

        def hand_over():
            @pl.when((layer == 0) & (core == 0))
            def _():
                pl.semaphore_signal(turn, inc=1, device_id=sibling, device_id_type=MESH)

        steps["turn"] = hand_over
        for step in SCHEDULE:
            name, *places = step.split()
            steps[name](*[int(place) for place in places])
        return carry

    lax.fori_loop(0, 2, one_layer, 0)
    last = remote(results.at[1 - core], out.at[core], pair_send.at[5], pair_recv.at[5], sibling)
    last.start()
    keep = pltpu.make_async_copy(results.at[core], out.at[core], local_sem.at[0])
    keep.start()
    keep.wait()
    last.wait()


def shards(tokens, norm_gain, expert_gate, expert_up, expert_down, routes, route_weights):
    named = jnp.swapaxes(routes[0], 1, 2)
    weight = jnp.swapaxes(route_weights[0], 1, 2)
    anywhere = pl.BlockSpec(memory_space=pl.ANY)
    dma = pltpu.SemaphoreType.DMA
    out = pl.pallas_call(
        kernel,
        out_shape=jax.ShapeDtypeStruct((2, TOK, Q), BF),
        in_specs=[anywhere] * 7,
        out_specs=anywhere,
        scratch_shapes=[
            pltpu.VMEM((2, D, FFQ), BF),
            pltpu.VMEM((2, D, FFQ), BF),
            pltpu.VMEM((2, FFQ, D), BF),
            pltpu.VMEM((2, 1, D), F32),
            pltpu.VMEM((2, NZ, TOK, Q), BF),
            pltpu.VMEM((2, TOPK, TOK), jnp.int32),
            pltpu.VMEM((2, TOPK, TOK), F32),
            pltpu.VMEM((2, 2 * TOPK, 128), BF),
            pltpu.VMEM((NZ, 2, 2 * TOPK, 128), BF),
            pltpu.VMEM((2, GROUPS, WIDE, Q), BF),
            pltpu.VMEM((2, GROUPS, 4, WIDE, Q), BF),
            pltpu.VMEM((2, GROUPS, 4, WIDE, Q), BF),
            pltpu.VMEM((2, GROUPS, 3, WIDE, Q), BF),
            pltpu.VMEM((2, GROUPS, WIDE, Q), BF),
            pltpu.VMEM((2, GROUPS, WIDE, Q), BF),
            pltpu.VMEM((2, GROUPS, WIDE, Q), BF),
            pltpu.VMEM((2, GROUPS, WIDE, 512), BF),
            pltpu.VMEM((2, len(MIXES), WIDE, 128), BF),
            pltpu.VMEM((2, NZ, TOK, Q), BF),
            pltpu.VMEM((2, NZ, TOK, Q), BF),
            pltpu.VMEM((2, TOK, Q), BF),
            dma((7,)),
            dma((6,)),
            dma((6,)),
            dma((2, NZ)),
            dma((2, NZ)),
            dma((NZ,)),
            dma((NZ,)),
            dma((2, GROUPS, NY)),
            dma((2, GROUPS, NY)),
            dma((2, GROUPS, NY)),
            dma((2, GROUPS, NY)),
            dma((2, GROUPS, 2, 3)),
            dma((2, GROUPS, 2, 3)),
            dma((2, GROUPS, 2, 3)),
            dma((2, GROUPS, 2, 3)),
            dma((2, NZ)),
            dma((2, NZ)),
            pltpu.SemaphoreType.REGULAR,
        ],
        compiler_params=pltpu.CompilerParams(
            collective_id=0, has_side_effects=True, vmem_limit_bytes=56 * 1024 * 1024
        ),
        cost_estimate=pl.CostEstimate(
            flops=2 * 2 * 576 * D * 768, bytes_accessed=8 * 1024 * 1024, transcendentals=0
        ),
    )(tokens, norm_gain, named, weight, expert_gate[0, 0], expert_up[0, 0], expert_down[0, 0])
    return out[None]


def solution(mesh):
    placed = (
        P(None, "ep", "tp"),
        P("section", None),
        P("section", "ep", None, "tp"),
        P("section", "ep", None, "tp"),
        P("section", "ep", "tp", None),
        P("section", None, "ep", None),
        P("section", None, "ep", None),
    )
    return jax.shard_map(
        shards,
        mesh=mesh,
        in_specs=placed,
        out_specs=P("section", None, "ep", "tp"),
        check_vma=False,
    )
```

```python
import jax
import jax.numpy as jnp
from jax import lax
from jax.experimental import pallas as pl
from jax.experimental.pallas import tpu as pltpu
from jax.sharding import PartitionSpec as P

EPSILON = 1e-06
NZ, NY, NX = 16, 4, 4
TOK, TOPK, CAP = 64, 8, 9
D, Q, FFQ = 2048, 512, 256
ROWS = NZ * CAP
MESH = pl.DeviceIdType.MESH
PLACE = (0, 1, 15, 2, 14, 3, 13, 4, 12, 6, 10, 5, 11, 7, 9, 8)
AT = {distance: p for p, distance in enumerate(PLACE)}
PARENT = {
    3: (0, -3), 13: (0, 3), 2: (0, -2), 14: (0, 2), 1: (0, -1), 15: (0, 1),
    6: (3, -3), 4: (3, -1), 5: (3, -2), 10: (13, 3), 12: (13, 1),
    7: (6, -1), 8: (10, 2), 9: (10, 1), 11: (10, -1),
}
CHILDREN = {
    root: [child for child, (parent, _) in PARENT.items() if parent == root]
    for root in (0, 3, 13, 6, 10)
}
GROUPS = 3
PART = ROWS // GROUPS
PAIRS = tuple(range(g * PART // (2 * CAP), -(-(g + 1) * PART // (2 * CAP))) for g in range(GROUPS))
MIXES = tuple((q, g) for g in range(GROUPS) for q in PAIRS[g])
TURN = (0, 1, 3, 2)
WIDE = NY * PART
HALF = WIDE // 2
DIRECT = (False, False, True)
BF, F32 = jnp.bfloat16, jnp.float32

SCHEDULE = (
    "hold", "z 0", "z 13", "z 3", "zw 14", "zw 15", "zw 1", "b 2", "zw 2", "b 0", "b 1",
    "s 0", "z 10", "z 6", "zw 12", "zw 4", "xs 0 0", "b 3", "zw 5", "b 4", "b 5", "s 1",
    "xs 0 1", "zw 11", "zw 8", "zw 7", "w", "b 6", "zw 9", "b 7", "s 2", "xs 1 0", "xp 0 0",
    "xp 0 1", "xs 1 1", "xs 2 1", "bn", "xp 1 0", "xp 1 1", "xs 2 0", "xp 2 1", "e 2 1",
    "e 1 0", "turn", "e 1 1", "f 2 1", "xp 2 0", "e 2 0", "f 2 0", "d 2 1", "f 1 0",
    "f 1 1", "e 0 1", "e 0 0", "d 2 0", "d 1 1", "d 1 0", "f 0 1", "f 0 0", "r 2", "c 7",
    "c 6", "r 1", "c 3", "d 0 1", "c 5", "d 0 0", "c 4", "p 6", "p 10", "r 0", "c 0", "c 1",
    "c 2", "p 3", "p 13", "settle", "last",
)


def remote(src, dst, send, recv, device):
    return pltpu.make_async_remote_copy(
        src_ref=src,
        dst_ref=dst,
        send_sem=send,
        recv_sem=recv,
        device_id=device,
        device_id_type=MESH,
    )


def kernel(
    tokens,
    gain_in,
    named_in,
    weight_in,
    gate_in,
    up_in,
    down_in,
    out,
    gate,
    up,
    down,
    gains,
    blocks,
    named,
    weight,
    own_meta,
    meta,
    chosen,
    rows,
    parts,
    half,
    half_out,
    done,
    back,
    pick,
    mix,
    ring_out,
    ring_in,
    results,
    local_sem,
    pair_send,
    pair_recv,
    zg_send,
    zg_recv,
    zm_send,
    zm_recv,
    yg_send,
    yg_recv,
    yr_send,
    yr_recv,
    xg_send,
    xg_recv,
    xr_send,
    xr_recv,
    zr_send,
    zr_recv,
    turn,
):
    core = lax.axis_index("section")
    x = lax.axis_index("tp")
    ep = lax.axis_index("ep")
    z, y = ep // NY, ep % NY
    sibling = (1 - core, x, ep)

    def at_z(step):
        return (core, x, ((z + step + NZ) % NZ) * NY + y)

    def at_y(step):
        return (core, x, z * NY + (y + step + NY) % NY)

    x_one = x + 1 - 2 * (x % 2)
    x_three = 3 - x
    x_two = (x + 2) % 4
    quarter = (x, x_one, x_two, x_three)

    def at_x(which):
        return (core, which, ep)

    def pair_copies():
        sources = (
            (own_meta.at[1 - core], meta.at[0, core]),
            (gain_in, gains.at[core]),
            (gate_in, gate.at[core]),
            (up_in, up.at[core]),
            (down_in, down.at[core]),
        )
        return [
            remote(src, dst, pair_send.at[n], pair_recv.at[n], sibling)
            for n, (src, dst) in enumerate(sources)
        ]

    def own_copies():
        sources = (
            (tokens.at[core], blocks.at[0, 0]),
            (named_in, named),
            (weight_in, weight),
            (gain_in, gains.at[core]),
            (gate_in, gate.at[core]),
            (up_in, up.at[core]),
            (down_in, down.at[core]),
        )
        return [
            pltpu.make_async_copy(src, dst, local_sem.at[n]) for n, (src, dst) in enumerate(sources)
        ]

    pair, own = pair_copies(), own_copies()
    for copy in own:
        copy.start()

    barrier = pltpu.get_barrier_semaphore()
    friends = [sibling, at_y(1), at_y(2), at_y(3), at_x(x_one), at_x(x_three)]
    if any(DIRECT):
        friends += [at_x(x_two)]
    friends += [at_z(step) for step in (-3, -2, -1, 1, 2, 3)]
    for friend in friends:
        pl.semaphore_signal(barrier, inc=1, device_id=friend, device_id_type=MESH)
    own[1].wait()
    own[2].wait()
    for micro in range(2):
        entry = jnp.concatenate([named[micro].astype(F32), weight[micro]], axis=0)
        own_meta[micro] = jnp.concatenate([entry, entry], axis=1).astype(BF)
    meta[0, core] = own_meta[core]
    own[0].wait()
    pl.semaphore_wait(barrier, len(friends))

    for copy in pair:
        copy.start()

    def gather(layer, distance):
        parent, step = PARENT[distance]
        p = AT[distance]
        return remote(
            blocks.at[layer, AT[parent]],
            blocks.at[layer, p],
            zg_send.at[layer, p],
            zg_recv.at[layer, p],
            at_z(step),
        )

    def gather_meta(distance):
        parent, step = PARENT[distance]
        p = AT[distance]
        return remote(meta.at[AT[parent]], meta.at[p], zm_send.at[p], zm_recv.at[p], at_z(step))

    def reduce(layer, distance):
        _, step = PARENT[distance]
        p = AT[distance]
        return remote(
            ring_out.at[layer, p],
            ring_in.at[layer, p],
            zr_send.at[layer, p],
            zr_recv.at[layer, p],
            at_z(-step),
        )

    def y_go(layer, g, k):
        return remote(
            chosen.at[layer, g, pl.ds(k * PART, PART)],
            rows.at[layer, g, 0, pl.ds(k * PART, PART)],
            yg_send.at[layer, g, k],
            yg_recv.at[layer, g, k],
            at_y(TURN[k]),
        )

    def y_back(layer, g, k):
        return remote(
            done.at[layer, g, pl.ds(k * PART, PART)],
            back.at[layer, g, pl.ds(k * PART, PART)],
            yr_send.at[layer, g, k],
            yr_recv.at[layer, g, k],
            at_y(-TURN[k]),
        )

    def x_gather(layer, g, h):
        first, second = (1, 3) if h == 0 else (3, 1)
        span = pl.ds(h * HALF, HALF)
        source = 0 if DIRECT[g] else first
        far = 2 if DIRECT[g] else second
        return [
            remote(
                rows.at[layer, g, src, span],
                rows.at[layer, g, dst, span],
                xg_send.at[layer, g, h, n],
                xg_recv.at[layer, g, h, n],
                at_x(quarter[to]),
            )
            for n, (src, dst, to) in enumerate(
                ((0, first, first), (0, second, second), (source, 2, far))
            )
        ]

    def x_reduce(layer, g, h):
        first, second = (1, 3) if h == 0 else (3, 1)
        span = pl.ds(h * HALF, HALF)
        if DIRECT[g]:
            ways = [(parts.at[layer, g, n, span], n) for n in (2, 1, 3)]
        else:
            ways = [
                (parts.at[layer, g, 2, span], first),
                (parts.at[layer, g, first, span], first),
                (half_out.at[layer, g, span], second),
            ]
        return [
            remote(
                src,
                half.at[layer, g, n, span],
                xr_send.at[layer, g, h, n],
                xr_recv.at[layer, g, h, n],
                at_x(quarter[to]),
            )
            for n, (src, to) in enumerate(ways)
        ]

    def build_selection(layer, pairs):
        lane = lax.broadcasted_iota(jnp.int32, (2 * TOPK, 128), 1)
        low = lane < TOK
        a = lax.broadcasted_iota(jnp.int32, (128, 128), 0)
        b = lax.broadcasted_iota(jnp.int32, (128, 128), 1)
        before = jnp.where((a < b) & ((a < TOK) == (b < TOK)), 1.0, 0.0).astype(BF)
        row_number = lax.broadcasted_iota(jnp.int32, (PART, 128), 0).astype(F32)
        high_one = jnp.where(lax.broadcasted_iota(jnp.int32, (1, 128), 1) < TOK, 0.0, 1.0)
        for q in pairs:
            entry = jnp.where(
                low, meta[2 * q, layer].astype(F32), meta[2 * q + 1, layer].astype(F32)
            )
            named, weight = entry[:TOPK], entry[TOPK:]
            same = [
                jnp.where(named == (z * NY + (y + TURN[k]) % NY).astype(F32), 1.0, 0.0)
                for k in range(NY)
            ]
            count = jnp.dot(
                jnp.concatenate(same, axis=0).astype(BF), before, preferred_element_type=F32
            )
            for k in range(NY):
                position = jnp.sum(count[k * TOPK : (k + 1) * TOPK], axis=0, keepdims=True)
                hits = jnp.sum(same[k], axis=0, keepdims=True)
                share = jnp.sum(same[k] * weight, axis=0, keepdims=True)
                slot = jnp.where(hits > 0.5, position + CAP * (2 * q + high_one), -1.0)
                for m, (other, g) in enumerate(MIXES):
                    if other == q:
                        hit = row_number + g * PART == slot
                        at = (q - PAIRS[g][0]) * 128
                        pick[layer, g, k * PART : (k + 1) * PART, at : at + 128] = jnp.where(
                            hit, 1.0, 0.0
                        ).astype(BF)
                        mix[layer, m, k * PART : (k + 1) * PART, :] = jnp.where(
                            hit, share, 0.0
                        ).astype(BF)

    def expert(layer, g, h):
        span_rows = slice(h * HALF, (h + 1) * HALF)
        total = jnp.zeros((HALF, 1), F32)
        for s in range(4):
            value = rows[layer, g, s, span_rows].astype(F32)
            total = total + jnp.sum(value * value, axis=1, keepdims=True)
        scale = lax.rsqrt(total / D + EPSILON)
        gate_act = jnp.zeros((HALF, FFQ), F32)
        up_act = jnp.zeros((HALF, FFQ), F32)
        for s in range(4):
            span = pl.ds(pl.multiple_of(quarter[s] * Q, Q), Q)
            value = rows[layer, g, s, span_rows].astype(F32)
            normed = (value * scale * gains[layer, 0:1, span]).astype(BF)
            gate_act += jnp.dot(normed, gate[layer, span, :], preferred_element_type=F32)
            up_act += jnp.dot(normed, up[layer, span, :], preferred_element_type=F32)
        hidden = (gate_act / (1.0 + jnp.exp(-gate_act)) * up_act).astype(BF)
        sends = x_reduce(layer, g, h)
        first = 1 if h == 0 else 3
        order = (2, 1, 3, 0) if DIRECT[g] else (2, first, 4 - first, 0)
        for n, s in enumerate(order):
            span = pl.ds(pl.multiple_of(quarter[s] * Q, Q), Q)
            parts[layer, g, s, span_rows] = jnp.dot(
                hidden, down[layer, :, span], preferred_element_type=F32
            ).astype(BF)
            if n < (3 if DIRECT[g] else 2):
                sends[n].start()

    across = remote(results.at[1 - core], out.at[core], pair_send.at[5], pair_recv.at[5], sibling)
    keep = pltpu.make_async_copy(results.at[core], out.at[core], local_sem.at[0])

    def one_layer(layer, carry):
        sums = {}

        def first_only(action):
            pl.when(layer == 0)(action)

        def z_pass(root):
            if root:
                gather(layer, root).wait_recv()
            for distance in CHILDREN[root]:
                gather(layer, distance).start()

            @first_only
            def _():
                if root:
                    gather_meta(root).wait_recv()
                else:
                    pair[0].wait()
                for distance in CHILDREN[root]:
                    gather_meta(distance).start()

        def z_wait(*distances):
            for distance in distances:
                gather(layer, distance).wait_recv()

            @first_only
            def _():
                for distance in distances:
                    gather_meta(distance).wait_recv()

        def build(*pairs):
            first_only(lambda: build_selection(0, pairs))

        def build_next():
            first_only(lambda: build_selection(1, range(NZ // 2)))

        def select(g):
            pairs = PAIRS[g]
            source = blocks[layer, 2 * pairs[0] : 2 * pairs[-1] + 2].reshape(-1, Q)
            value = jnp.dot(
                pick[layer, g, :, 0 : len(pairs) * 128], source, preferred_element_type=F32
            ).astype(BF)
            chosen[layer, g] = value
            for k in (1, 2, 3):
                y_go(layer, g, k).start()
            rows[layer, g, 0, 0:PART] = value[:PART]

        def x_send(g, h):
            for k in (2 * h, 2 * h + 1):
                if k:
                    y_go(layer, g, k).wait_recv()
            copies = x_gather(layer, g, h)
            for copy in copies if DIRECT[g] else copies[:2]:
                copy.start()

        def x_pass(g, h):
            copies = x_gather(layer, g, h)
            copies[0].wait_recv()
            if not DIRECT[g]:
                copies[2].start()

        def weights():
            @first_only
            def _():
                for copy in pair[1:] + own[3:]:
                    copy.wait()

        def work(g, h):
            copies = x_gather(layer, g, h)
            copies[1].wait_recv()
            copies[2].wait_recv()
            expert(layer, g, h)

        def fold(g, h):
            if not DIRECT[g]:
                span = slice(h * HALF, (h + 1) * HALF)
                copies = x_reduce(layer, g, h)
                copies[0].wait_recv()
                half_out[layer, g, span] = (
                    parts[layer, g, 3 - 2 * h, span].astype(F32)
                    + half[layer, g, 0, span].astype(F32)
                ).astype(BF)
                copies[2].start()

        def finish(g, h):
            span = slice(h * HALF, (h + 1) * HALF)
            copies = x_reduce(layer, g, h)
            terms = (0, 1, 2) if DIRECT[g] else (1, 2)
            for n in terms:
                copies[n].wait_recv()
            value = parts[layer, g, 0, span].astype(F32)
            for n in terms:
                value = value + half[layer, g, n, span].astype(F32)
            value = value.astype(BF)
            done[layer, g, span] = value
            for k in (2 * h, 2 * h + 1):
                if k:
                    y_back(layer, g, k).start()
            if h == 0:
                back[layer, g, 0:PART] = value[:PART]

        def returned(g):
            for k in (1, 2, 3):
                y_back(layer, g, k).wait_recv()

        def collect(distance, value):
            for child in CHILDREN.get(distance, ()):
                reduce(layer, child).wait_recv()
                value = value + ring_in[layer, AT[child]].astype(F32)
            return value

        def pass_on(distance):
            ring_out[layer, AT[distance]] = collect(distance, sums[distance]).astype(BF)
            reduce(layer, distance).start()

        def combine(q):
            value = None
            for m, (other, g) in enumerate(MIXES):
                if other == q:
                    term = lax.dot_general(
                        mix[layer, m],
                        back[layer, g],
                        (((0,), (0,)), ((), ())),
                        preferred_element_type=F32,
                    )
                    value = term if value is None else value + term
            for k in range(2):
                distance = PLACE[2 * q + k]
                sums[distance] = value[k * TOK : (k + 1) * TOK]
                if distance not in CHILDREN:
                    pass_on(distance)

        def settle():
            for distance in PLACE[1:]:
                gather(layer, distance).wait_send()
                if distance not in (3, 13):
                    reduce(layer, distance).wait_send()

            @first_only
            def _():
                for distance in PLACE[1:]:
                    gather_meta(distance).wait_send()

            for g in range(GROUPS):
                for k in (1, 2, 3):
                    y_go(layer, g, k).wait_send()
                    y_back(layer, g, k).wait_send()
                for h in range(2):
                    for copy in x_gather(layer, g, h) + x_reduce(layer, g, h):
                        copy.wait_send()

        def last():
            for distance in (3, 13):
                reduce(layer, distance).wait_send()
            final = collect(0, sums[0] + blocks[layer, 0].astype(F32)).astype(BF)
            results[layer] = final

            @first_only
            def _():
                blocks[1, 0] = final

            pl.when(layer == core)(keep.start)
            pl.when(layer != core)(across.start)

        steps = dict(
            z=z_pass, zw=z_wait, b=build, bn=build_next, s=select, xs=x_send, xp=x_pass,
            w=weights, e=work, f=fold, d=finish, r=returned, c=combine, p=pass_on,
            settle=settle, last=last,
        )
        def hold():
            @pl.when((layer == 0) & (core == 1))
            def _():
                pl.semaphore_wait(turn, 1)

        def hand_over():
            @pl.when((layer == 0) & (core == 0))
            def _():
                pl.semaphore_signal(turn, inc=1, device_id=sibling, device_id_type=MESH)

        steps["turn"] = hand_over
        steps["hold"] = hold
        for step in SCHEDULE:
            name, *places = step.split()
            steps[name](*[int(place) for place in places])
        return carry

    lax.fori_loop(0, 2, one_layer, 0)
    across.wait()
    keep.wait()


def shards(tokens, norm_gain, expert_gate, expert_up, expert_down, routes, route_weights):
    named = jnp.swapaxes(routes[0], 1, 2)
    weight = jnp.swapaxes(route_weights[0], 1, 2)
    anywhere = pl.BlockSpec(memory_space=pl.ANY)
    dma = pltpu.SemaphoreType.DMA
    out = pl.pallas_call(
        kernel,
        out_shape=jax.ShapeDtypeStruct((2, TOK, Q), BF),
        in_specs=[anywhere] * 7,
        out_specs=anywhere,
        scratch_shapes=[
            pltpu.VMEM((2, D, FFQ), BF),
            pltpu.VMEM((2, D, FFQ), BF),
            pltpu.VMEM((2, FFQ, D), BF),
            pltpu.VMEM((2, 1, D), F32),
            pltpu.VMEM((2, NZ, TOK, Q), BF),
            pltpu.VMEM((2, TOPK, TOK), jnp.int32),
            pltpu.VMEM((2, TOPK, TOK), F32),
            pltpu.VMEM((2, 2 * TOPK, 128), BF),
            pltpu.VMEM((NZ, 2, 2 * TOPK, 128), BF),
            pltpu.VMEM((2, GROUPS, WIDE, Q), BF),
            pltpu.VMEM((2, GROUPS, 4, WIDE, Q), BF),
            pltpu.VMEM((2, GROUPS, 4, WIDE, Q), BF),
            pltpu.VMEM((2, GROUPS, 3, WIDE, Q), BF),
            pltpu.VMEM((2, GROUPS, WIDE, Q), BF),
            pltpu.VMEM((2, GROUPS, WIDE, Q), BF),
            pltpu.VMEM((2, GROUPS, WIDE, Q), BF),
            pltpu.VMEM((2, GROUPS, WIDE, 512), BF),
            pltpu.VMEM((2, len(MIXES), WIDE, 128), BF),
            pltpu.VMEM((2, NZ, TOK, Q), BF),
            pltpu.VMEM((2, NZ, TOK, Q), BF),
            pltpu.VMEM((2, TOK, Q), BF),
            dma((7,)),
            dma((6,)),
            dma((6,)),
            dma((2, NZ)),
            dma((2, NZ)),
            dma((NZ,)),
            dma((NZ,)),
            dma((2, GROUPS, NY)),
            dma((2, GROUPS, NY)),
            dma((2, GROUPS, NY)),
            dma((2, GROUPS, NY)),
            dma((2, GROUPS, 2, 3)),
            dma((2, GROUPS, 2, 3)),
            dma((2, GROUPS, 2, 3)),
            dma((2, GROUPS, 2, 3)),
            dma((2, NZ)),
            dma((2, NZ)),
            pltpu.SemaphoreType.REGULAR,
        ],
        compiler_params=pltpu.CompilerParams(
            collective_id=0, has_side_effects=True, vmem_limit_bytes=56 * 1024 * 1024
        ),
        cost_estimate=pl.CostEstimate(
            flops=2 * 2 * 576 * D * 768, bytes_accessed=8 * 1024 * 1024, transcendentals=0
        ),
    )(tokens, norm_gain, named, weight, expert_gate[0, 0], expert_up[0, 0], expert_down[0, 0])
    return out[None]


def solution(mesh):
    placed = (
        P(None, "ep", "tp"),
        P("section", None),
        P("section", "ep", None, "tp"),
        P("section", "ep", None, "tp"),
        P("section", "ep", "tp", None),
        P("section", None, "ep", None),
        P("section", None, "ep", None),
    )
    return jax.shard_map(
        shards,
        mesh=mesh,
        in_specs=placed,
        out_specs=P("section", None, "ep", "tp"),
        check_vma=False,
    )
```

```python
import jax
import jax.numpy as jnp
from jax import lax
from jax.experimental import pallas as pl
from jax.experimental.pallas import tpu as pltpu
from jax.sharding import PartitionSpec as P

EPSILON = 1e-06
NZ, NY, NX = 16, 4, 4
TOK, TOPK, CAP = 64, 8, 9
D, Q, FFQ = 2048, 512, 256
ROWS = NZ * CAP
MESH = pl.DeviceIdType.MESH
PLACE = (0, 1, 15, 2, 14, 3, 13, 4, 12, 6, 10, 5, 11, 7, 9, 8)
AT = {distance: p for p, distance in enumerate(PLACE)}
PARENT = {
    3: (0, -3), 13: (0, 3), 2: (0, -2), 14: (0, 2), 1: (0, -1), 15: (0, 1),
    6: (3, -3), 4: (3, -1), 5: (3, -2), 10: (13, 3), 12: (13, 1),
    7: (6, -1), 8: (10, 2), 9: (10, 1), 11: (10, -1),
}
CHILDREN = {
    root: [child for child, (parent, _) in PARENT.items() if parent == root]
    for root in (0, 3, 13, 6, 10)
}
GROUPS = 3
PART = ROWS // GROUPS
PAIRS = tuple(range(g * PART // (2 * CAP), -(-(g + 1) * PART // (2 * CAP))) for g in range(GROUPS))
MIXES = tuple((q, g) for g in range(GROUPS) for q in PAIRS[g])
TURN = (0, 1, 3, 2)
WIDE = NY * PART
HALF = WIDE // 2
PIECES = 2
PIECE = TOK // PIECES
DIRECT = (False, False, True)
BF, F32 = jnp.bfloat16, jnp.float32

SCHEDULE = (
    "hold", "z 0", "z 3 13", "zw 14", "zw 15", "zw 1", "b 2", "zw 2", "b 0", "b 1", "s 0",
    "z 6 10", "zw 12", "zw 4", "xs 0 0", "b 3", "zw 5", "b 4", "b 5", "s 1", "xs 0 1",
    "zw 11", "zw 8", "zw 7", "w", "b 6", "zw 9", "b 7", "s 2", "xs 1 0", "xp 0 0", "xp 0 1",
    "xs 1 1", "xs 2 1", "bn", "xp 1 0", "xp 1 1", "xs 2 0", "xp 2 1", "e 2 1", "e 1 0",
    "e 1 1", "turn", "f 2 1", "xp 2 0", "e 2 0", "f 2 0", "d 2 1", "f 1 0", "f 1 1",
    "e 0 1", "e 0 0", "d 2 0", "d 1 1", "d 1 0", "f 0 1", "f 0 0", "r 2", "c 7", "c 6",
    "r 1", "c 3", "d 0 1", "c 5", "d 0 0", "c 4", "p 6 10", "r 0", "c 0", "c 1", "c 2",
    "p 3 13", "settle", "last",
)


def remote(src, dst, send, recv, device):
    return pltpu.make_async_remote_copy(
        src_ref=src,
        dst_ref=dst,
        send_sem=send,
        recv_sem=recv,
        device_id=device,
        device_id_type=MESH,
    )


def kernel(
    tokens,
    gain_in,
    named_in,
    weight_in,
    gate_in,
    up_in,
    down_in,
    out,
    gate,
    up,
    down,
    gains,
    blocks,
    named,
    weight,
    own_meta,
    meta,
    chosen,
    rows,
    parts,
    half,
    half_out,
    done,
    back,
    pick,
    mix,
    ring_out,
    ring_in,
    results,
    local_sem,
    pair_send,
    pair_recv,
    zg_send,
    zg_recv,
    zm_send,
    zm_recv,
    yg_send,
    yg_recv,
    yr_send,
    yr_recv,
    xg_send,
    xg_recv,
    xr_send,
    xr_recv,
    zr_send,
    zr_recv,
    turn,
):
    core = lax.axis_index("section")
    x = lax.axis_index("tp")
    ep = lax.axis_index("ep")
    z, y = ep // NY, ep % NY
    sibling = (1 - core, x, ep)

    def at_z(step):
        return (core, x, ((z + step + NZ) % NZ) * NY + y)

    def at_y(step):
        return (core, x, z * NY + (y + step + NY) % NY)

    x_one = x + 1 - 2 * (x % 2)
    x_three = 3 - x
    x_two = (x + 2) % 4
    quarter = (x, x_one, x_two, x_three)

    def at_x(which):
        return (core, which, ep)

    def pair_copies():
        sources = (
            (own_meta.at[1 - core], meta.at[0, core]),
            (gain_in, gains.at[core]),
            (gate_in, gate.at[core]),
            (up_in, up.at[core]),
            (down_in, down.at[core]),
        )
        return [
            remote(src, dst, pair_send.at[n], pair_recv.at[n], sibling)
            for n, (src, dst) in enumerate(sources)
        ]

    def own_copies():
        sources = (
            (tokens.at[core], blocks.at[0, 0]),
            (named_in, named),
            (weight_in, weight),
            (gain_in, gains.at[core]),
            (gate_in, gate.at[core]),
            (up_in, up.at[core]),
            (down_in, down.at[core]),
        )
        return [
            pltpu.make_async_copy(src, dst, local_sem.at[n]) for n, (src, dst) in enumerate(sources)
        ]

    pair, own = pair_copies(), own_copies()
    for copy in own:
        copy.start()

    barrier = pltpu.get_barrier_semaphore()
    friends = [sibling, at_y(1), at_y(2), at_y(3), at_x(x_one), at_x(x_three)]
    if any(DIRECT):
        friends += [at_x(x_two)]
    friends += [at_z(step) for step in (-3, -2, -1, 1, 2, 3)]
    for friend in friends:
        pl.semaphore_signal(barrier, inc=1, device_id=friend, device_id_type=MESH)
    own[1].wait()
    own[2].wait()
    for micro in range(2):
        entry = jnp.concatenate([named[micro].astype(F32), weight[micro]], axis=0)
        own_meta[micro] = jnp.concatenate([entry, entry], axis=1).astype(BF)
    meta[0, core] = own_meta[core]
    own[0].wait()
    pl.semaphore_wait(barrier, len(friends))

    for copy in pair:
        copy.start()

    def gather(layer, distance, piece):
        parent, step = PARENT[distance]
        p = AT[distance]
        span = pl.ds(piece * PIECE, PIECE)
        return remote(
            blocks.at[layer, AT[parent], span],
            blocks.at[layer, p, span],
            zg_send.at[layer, p, piece],
            zg_recv.at[layer, p, piece],
            at_z(step),
        )

    def gather_meta(distance):
        parent, step = PARENT[distance]
        p = AT[distance]
        return remote(meta.at[AT[parent]], meta.at[p], zm_send.at[p], zm_recv.at[p], at_z(step))

    def reduce(layer, distance, piece):
        _, step = PARENT[distance]
        p = AT[distance]
        span = pl.ds(piece * PIECE, PIECE)
        return remote(
            ring_out.at[layer, p, span],
            ring_in.at[layer, p, span],
            zr_send.at[layer, p, piece],
            zr_recv.at[layer, p, piece],
            at_z(-step),
        )

    def y_go(layer, g, k):
        return remote(
            chosen.at[layer, g, pl.ds(k * PART, PART)],
            rows.at[layer, g, 0, pl.ds(k * PART, PART)],
            yg_send.at[layer, g, k],
            yg_recv.at[layer, g, k],
            at_y(TURN[k]),
        )

    def y_back(layer, g, k):
        return remote(
            done.at[layer, g, pl.ds(k * PART, PART)],
            back.at[layer, g, pl.ds(k * PART, PART)],
            yr_send.at[layer, g, k],
            yr_recv.at[layer, g, k],
            at_y(-TURN[k]),
        )

    def x_gather(layer, g, h):
        first, second = (1, 3) if h == 0 else (3, 1)
        span = pl.ds(h * HALF, HALF)
        source = 0 if DIRECT[g] else first
        far = 2 if DIRECT[g] else second
        return [
            remote(
                rows.at[layer, g, src, span],
                rows.at[layer, g, dst, span],
                xg_send.at[layer, g, h, n],
                xg_recv.at[layer, g, h, n],
                at_x(quarter[to]),
            )
            for n, (src, dst, to) in enumerate(
                ((0, first, first), (0, second, second), (source, 2, far))
            )
        ]

    def x_reduce(layer, g, h):
        first, second = (1, 3) if h == 0 else (3, 1)
        span = pl.ds(h * HALF, HALF)
        if DIRECT[g]:
            ways = [(parts.at[layer, g, n, span], n) for n in (2, 1, 3)]
        else:
            ways = [
                (parts.at[layer, g, 2, span], first),
                (parts.at[layer, g, first, span], first),
                (half_out.at[layer, g, span], second),
            ]
        return [
            remote(
                src,
                half.at[layer, g, n, span],
                xr_send.at[layer, g, h, n],
                xr_recv.at[layer, g, h, n],
                at_x(quarter[to]),
            )
            for n, (src, to) in enumerate(ways)
        ]

    def build_selection(layer, pairs):
        lane = lax.broadcasted_iota(jnp.int32, (2 * TOPK, 128), 1)
        low = lane < TOK
        a = lax.broadcasted_iota(jnp.int32, (128, 128), 0)
        b = lax.broadcasted_iota(jnp.int32, (128, 128), 1)
        before = jnp.where((a < b) & ((a < TOK) == (b < TOK)), 1.0, 0.0).astype(BF)
        row_number = lax.broadcasted_iota(jnp.int32, (PART, 128), 0).astype(F32)
        high_one = jnp.where(lax.broadcasted_iota(jnp.int32, (1, 128), 1) < TOK, 0.0, 1.0)
        for q in pairs:
            entry = jnp.where(
                low, meta[2 * q, layer].astype(F32), meta[2 * q + 1, layer].astype(F32)
            )
            named, weight = entry[:TOPK], entry[TOPK:]
            same = [
                jnp.where(named == (z * NY + (y + TURN[k]) % NY).astype(F32), 1.0, 0.0)
                for k in range(NY)
            ]
            count = jnp.dot(
                jnp.concatenate(same, axis=0).astype(BF), before, preferred_element_type=F32
            )
            for k in range(NY):
                position = jnp.sum(count[k * TOPK : (k + 1) * TOPK], axis=0, keepdims=True)
                hits = jnp.sum(same[k], axis=0, keepdims=True)
                share = jnp.sum(same[k] * weight, axis=0, keepdims=True)
                slot = jnp.where(hits > 0.5, position + CAP * (2 * q + high_one), -1.0)
                for m, (other, g) in enumerate(MIXES):
                    if other == q:
                        hit = row_number + g * PART == slot
                        at = (q - PAIRS[g][0]) * 128
                        pick[layer, g, k * PART : (k + 1) * PART, at : at + 128] = jnp.where(
                            hit, 1.0, 0.0
                        ).astype(BF)
                        mix[layer, m, k * PART : (k + 1) * PART, :] = jnp.where(
                            hit, share, 0.0
                        ).astype(BF)

    def expert(layer, g, h):
        span_rows = slice(h * HALF, (h + 1) * HALF)
        total = jnp.zeros((HALF, 1), F32)
        for s in range(4):
            value = rows[layer, g, s, span_rows].astype(F32)
            total = total + jnp.sum(value * value, axis=1, keepdims=True)
        scale = lax.rsqrt(total / D + EPSILON)
        gate_act = jnp.zeros((HALF, FFQ), F32)
        up_act = jnp.zeros((HALF, FFQ), F32)
        for s in range(4):
            span = pl.ds(pl.multiple_of(quarter[s] * Q, Q), Q)
            value = rows[layer, g, s, span_rows].astype(F32)
            normed = (value * scale * gains[layer, 0:1, span]).astype(BF)
            gate_act += jnp.dot(normed, gate[layer, span, :], preferred_element_type=F32)
            up_act += jnp.dot(normed, up[layer, span, :], preferred_element_type=F32)
        hidden = (gate_act / (1.0 + jnp.exp(-gate_act)) * up_act).astype(BF)
        sends = x_reduce(layer, g, h)
        first = 1 if h == 0 else 3
        order = (2, 1, 3, 0) if DIRECT[g] else (2, first, 4 - first, 0)
        for n, s in enumerate(order):
            span = pl.ds(pl.multiple_of(quarter[s] * Q, Q), Q)
            parts[layer, g, s, span_rows] = jnp.dot(
                hidden, down[layer, :, span], preferred_element_type=F32
            ).astype(BF)
            if n < (3 if DIRECT[g] else 2):
                sends[n].start()

    across = remote(results.at[1 - core], out.at[core], pair_send.at[5], pair_recv.at[5], sibling)
    keep = pltpu.make_async_copy(results.at[core], out.at[core], local_sem.at[0])

    def one_layer(layer, carry):
        sums = {}

        def first_only(action):
            pl.when(layer == 0)(action)

        def z_pass(*roots):
            if roots == (0,):
                for distance in CHILDREN[0]:
                    for piece in range(PIECES):
                        gather(layer, distance, piece).start()
            else:
                for piece in range(PIECES):
                    for root in roots:
                        gather(layer, root, piece).wait_recv()
                        for distance in CHILDREN[root]:
                            gather(layer, distance, piece).start()

            @first_only
            def _():
                for root in roots:
                    if root:
                        gather_meta(root).wait_recv()
                    else:
                        pair[0].wait()
                    for distance in CHILDREN[root]:
                        gather_meta(distance).start()

        def z_wait(*distances):
            for distance in distances:
                for piece in range(PIECES):
                    gather(layer, distance, piece).wait_recv()

            @first_only
            def _():
                for distance in distances:
                    gather_meta(distance).wait_recv()

        def build(*pairs):
            first_only(lambda: build_selection(0, pairs))

        def build_next():
            first_only(lambda: build_selection(1, range(NZ // 2)))

        def select(g):
            pairs = PAIRS[g]
            source = blocks[layer, 2 * pairs[0] : 2 * pairs[-1] + 2].reshape(-1, Q)
            value = jnp.dot(
                pick[layer, g, :, 0 : len(pairs) * 128], source, preferred_element_type=F32
            ).astype(BF)
            chosen[layer, g] = value
            for k in (1, 2, 3):
                y_go(layer, g, k).start()
            rows[layer, g, 0, 0:PART] = value[:PART]

        def x_send(g, h):
            for k in (2 * h, 2 * h + 1):
                if k:
                    y_go(layer, g, k).wait_recv()
            copies = x_gather(layer, g, h)
            for copy in copies if DIRECT[g] else copies[:2]:
                copy.start()

        def x_pass(g, h):
            copies = x_gather(layer, g, h)
            copies[0].wait_recv()
            if not DIRECT[g]:
                copies[2].start()

        def weights():
            @first_only
            def _():
                for copy in pair[1:] + own[3:]:
                    copy.wait()

        def work(g, h):
            copies = x_gather(layer, g, h)
            copies[1].wait_recv()
            copies[2].wait_recv()
            expert(layer, g, h)

        def fold(g, h):
            if not DIRECT[g]:
                span = slice(h * HALF, (h + 1) * HALF)
                copies = x_reduce(layer, g, h)
                copies[0].wait_recv()
                half_out[layer, g, span] = (
                    parts[layer, g, 3 - 2 * h, span].astype(F32)
                    + half[layer, g, 0, span].astype(F32)
                ).astype(BF)
                copies[2].start()

        def finish(g, h):
            span = slice(h * HALF, (h + 1) * HALF)
            copies = x_reduce(layer, g, h)
            terms = (0, 1, 2) if DIRECT[g] else (1, 2)
            for n in terms:
                copies[n].wait_recv()
            value = parts[layer, g, 0, span].astype(F32)
            for n in terms:
                value = value + half[layer, g, n, span].astype(F32)
            value = value.astype(BF)
            done[layer, g, span] = value
            for k in (2 * h, 2 * h + 1):
                if k:
                    y_back(layer, g, k).start()
            if h == 0:
                back[layer, g, 0:PART] = value[:PART]

        def returned(g):
            for k in (1, 2, 3):
                y_back(layer, g, k).wait_recv()

        def collect(distance, piece, value):
            for child in CHILDREN.get(distance, ()):
                reduce(layer, child, piece).wait_recv()
                span = slice(piece * PIECE, (piece + 1) * PIECE)
                value = value + ring_in[layer, AT[child], span].astype(F32)
            return value

        def pass_on(*distances):
            for piece in range(PIECES):
                span = slice(piece * PIECE, (piece + 1) * PIECE)
                for distance in distances:
                    value = collect(distance, piece, sums[distance][span])
                    ring_out[layer, AT[distance], span] = value.astype(BF)
                    reduce(layer, distance, piece).start()

        def combine(q):
            value = None
            for m, (other, g) in enumerate(MIXES):
                if other == q:
                    term = lax.dot_general(
                        mix[layer, m],
                        back[layer, g],
                        (((0,), (0,)), ((), ())),
                        preferred_element_type=F32,
                    )
                    value = term if value is None else value + term
            for k in range(2):
                distance = PLACE[2 * q + k]
                sums[distance] = value[k * TOK : (k + 1) * TOK]
                if distance not in CHILDREN:
                    pass_on(distance)

        def settle():
            for distance in PLACE[1:]:
                for piece in range(PIECES):
                    gather(layer, distance, piece).wait_send()
                    if distance not in (3, 13):
                        reduce(layer, distance, piece).wait_send()

            @first_only
            def _():
                for distance in PLACE[1:]:
                    gather_meta(distance).wait_send()

            for g in range(GROUPS):
                for k in (1, 2, 3):
                    y_go(layer, g, k).wait_send()
                    y_back(layer, g, k).wait_send()
                for h in range(2):
                    for copy in x_gather(layer, g, h) + x_reduce(layer, g, h):
                        copy.wait_send()

        def last():
            for piece in range(PIECES):
                span = slice(piece * PIECE, (piece + 1) * PIECE)
                value = sums[0][span] + blocks[layer, 0, span].astype(F32)
                final = collect(0, piece, value).astype(BF)
                results[layer, span] = final

                @first_only
                def _():
                    blocks[1, 0, span] = final

                for distance in (3, 13):
                    reduce(layer, distance, piece).wait_send()

            pl.when(layer == core)(keep.start)
            pl.when(layer != core)(across.start)

        steps = dict(
            z=z_pass, zw=z_wait, b=build, bn=build_next, s=select, xs=x_send, xp=x_pass,
            w=weights, e=work, f=fold, d=finish, r=returned, c=combine, p=pass_on,
            settle=settle, last=last,
        )
        def hold():
            @pl.when((layer == 0) & (core == 1))
            def _():
                pl.semaphore_wait(turn, 1)

        def hand_over():
            @pl.when((layer == 0) & (core == 0))
            def _():
                pl.semaphore_signal(turn, inc=1, device_id=sibling, device_id_type=MESH)

        steps["turn"] = hand_over
        steps["hold"] = hold
        for step in SCHEDULE:
            name, *places = step.split()
            steps[name](*[int(place) for place in places])
        return carry

    lax.fori_loop(0, 2, one_layer, 0)
    across.wait()
    keep.wait()


def shards(tokens, norm_gain, expert_gate, expert_up, expert_down, routes, route_weights):
    named = jnp.swapaxes(routes[0], 1, 2)
    weight = jnp.swapaxes(route_weights[0], 1, 2)
    anywhere = pl.BlockSpec(memory_space=pl.ANY)
    dma = pltpu.SemaphoreType.DMA
    out = pl.pallas_call(
        kernel,
        out_shape=jax.ShapeDtypeStruct((2, TOK, Q), BF),
        in_specs=[anywhere] * 7,
        out_specs=anywhere,
        scratch_shapes=[
            pltpu.VMEM((2, D, FFQ), BF),
            pltpu.VMEM((2, D, FFQ), BF),
            pltpu.VMEM((2, FFQ, D), BF),
            pltpu.VMEM((2, 1, D), F32),
            pltpu.VMEM((2, NZ, TOK, Q), BF),
            pltpu.VMEM((2, TOPK, TOK), jnp.int32),
            pltpu.VMEM((2, TOPK, TOK), F32),
            pltpu.VMEM((2, 2 * TOPK, 128), BF),
            pltpu.VMEM((NZ, 2, 2 * TOPK, 128), BF),
            pltpu.VMEM((2, GROUPS, WIDE, Q), BF),
            pltpu.VMEM((2, GROUPS, 4, WIDE, Q), BF),
            pltpu.VMEM((2, GROUPS, 4, WIDE, Q), BF),
            pltpu.VMEM((2, GROUPS, 3, WIDE, Q), BF),
            pltpu.VMEM((2, GROUPS, WIDE, Q), BF),
            pltpu.VMEM((2, GROUPS, WIDE, Q), BF),
            pltpu.VMEM((2, GROUPS, WIDE, Q), BF),
            pltpu.VMEM((2, GROUPS, WIDE, 512), BF),
            pltpu.VMEM((2, len(MIXES), WIDE, 128), BF),
            pltpu.VMEM((2, NZ, TOK, Q), BF),
            pltpu.VMEM((2, NZ, TOK, Q), BF),
            pltpu.VMEM((2, TOK, Q), BF),
            dma((7,)),
            dma((6,)),
            dma((6,)),
            dma((2, NZ, PIECES)),
            dma((2, NZ, PIECES)),
            dma((NZ,)),
            dma((NZ,)),
            dma((2, GROUPS, NY)),
            dma((2, GROUPS, NY)),
            dma((2, GROUPS, NY)),
            dma((2, GROUPS, NY)),
            dma((2, GROUPS, 2, 3)),
            dma((2, GROUPS, 2, 3)),
            dma((2, GROUPS, 2, 3)),
            dma((2, GROUPS, 2, 3)),
            dma((2, NZ, PIECES)),
            dma((2, NZ, PIECES)),
            pltpu.SemaphoreType.REGULAR,
        ],
        compiler_params=pltpu.CompilerParams(
            collective_id=0, has_side_effects=True, vmem_limit_bytes=56 * 1024 * 1024
        ),
        cost_estimate=pl.CostEstimate(
            flops=2 * 2 * 576 * D * 768, bytes_accessed=8 * 1024 * 1024, transcendentals=0
        ),
    )(tokens, norm_gain, named, weight, expert_gate[0, 0], expert_up[0, 0], expert_down[0, 0])
    return out[None]


def solution(mesh):
    placed = (
        P(None, "ep", "tp"),
        P("section", None),
        P("section", "ep", None, "tp"),
        P("section", "ep", None, "tp"),
        P("section", "ep", "tp", None),
        P("section", None, "ep", None),
        P("section", None, "ep", None),
    )
    return jax.shard_map(
        shards,
        mesh=mesh,
        in_specs=placed,
        out_specs=P("section", None, "ep", "tp"),
        check_vma=False,
    )
```

```python
import jax
import jax.numpy as jnp
from jax import lax
from jax.experimental import pallas as pl
from jax.experimental.pallas import tpu as pltpu
from jax.sharding import PartitionSpec as P

EPSILON = 1e-06
NZ, NY, NX = 16, 4, 4
TOK, TOPK, CAP = 64, 8, 9
D, Q, FFQ = 2048, 512, 256
ROWS = NZ * CAP
MESH = pl.DeviceIdType.MESH
PLACE = (0, 1, 15, 2, 14, 3, 13, 4, 12, 6, 10, 5, 11, 7, 9, 8)
AT = {distance: p for p, distance in enumerate(PLACE)}
PARENT = {
    3: (0, -3), 13: (0, 3), 2: (0, -2), 14: (0, 2), 1: (0, -1), 15: (0, 1),
    6: (3, -3), 4: (3, -1), 5: (3, -2), 10: (13, 3), 12: (13, 1),
    7: (6, -1), 8: (10, 2), 9: (10, 1), 11: (10, -1),
}
CHILDREN = {
    root: [child for child, (parent, _) in PARENT.items() if parent == root]
    for root in (0, 3, 13, 6, 10)
}
GROUPS = 3
PART = ROWS // GROUPS
PAIRS = tuple(range(g * PART // (2 * CAP), -(-(g + 1) * PART // (2 * CAP))) for g in range(GROUPS))
MIXES = tuple((q, g) for g in range(GROUPS) for q in PAIRS[g])
TURN = (0, 1, 3, 2)
WIDE = NY * PART
HALF = WIDE // 2
PIECES = 2
PIECE = TOK // PIECES
DIRECT = (False, False, True)
BF, F32 = jnp.bfloat16, jnp.float32

SCHEDULE = (
    "hold", "z 0", "z 3 13", "zw 14", "zw 15", "zw 1", "b 2", "zw 2", "b 0", "b 1", "s 0",
    "z 6 10", "zw 12", "zw 4", "xs 0 0", "b 3", "zw 5", "b 4", "b 5", "s 1", "xs 0 1",
    "zw 11", "zw 8", "zw 7", "w", "b 6", "zw 9", "b 7", "s 2", "xs 1 0", "xp 0 0", "xp 0 1",
    "xs 1 1", "xs 2 1", "bn", "xp 1 0", "xp 1 1", "xs 2 0", "xp 2 1", "e 2 1", "e 1 0",
    "e 1 1", "f 2 1", "xp 2 0", "turn", "e 2 0", "f 2 0", "d 2 1", "f 1 0", "f 1 1",
    "e 0 1", "e 0 0", "d 2 0", "d 1 1", "d 1 0", "f 0 1", "f 0 0", "r 2", "c 7", "c 6",
    "r 1", "c 3", "d 0 1", "c 5", "d 0 0", "c 4", "p 6 10", "r 0", "c 0", "c 1", "c 2",
    "p 3 13", "settle", "last",
)


def remote(src, dst, send, recv, device):
    return pltpu.make_async_remote_copy(
        src_ref=src,
        dst_ref=dst,
        send_sem=send,
        recv_sem=recv,
        device_id=device,
        device_id_type=MESH,
    )


def kernel(
    tokens,
    gain_in,
    named_in,
    weight_in,
    gate_in,
    up_in,
    down_in,
    out,
    gate,
    up,
    down,
    gains,
    blocks,
    named,
    weight,
    own_meta,
    meta,
    chosen,
    rows,
    parts,
    half,
    half_out,
    done,
    back,
    pick,
    mix,
    ring_out,
    ring_in,
    results,
    local_sem,
    pair_send,
    pair_recv,
    zg_send,
    zg_recv,
    zm_send,
    zm_recv,
    yg_send,
    yg_recv,
    yr_send,
    yr_recv,
    xg_send,
    xg_recv,
    xr_send,
    xr_recv,
    zr_send,
    zr_recv,
    turn,
):
    core = lax.axis_index("section")
    x = lax.axis_index("tp")
    ep = lax.axis_index("ep")
    z, y = ep // NY, ep % NY
    sibling = (1 - core, x, ep)

    def at_z(step):
        return (core, x, ((z + step + NZ) % NZ) * NY + y)

    def at_y(step):
        return (core, x, z * NY + (y + step + NY) % NY)

    x_one = x + 1 - 2 * (x % 2)
    x_three = 3 - x
    x_two = (x + 2) % 4
    quarter = (x, x_one, x_two, x_three)

    def at_x(which):
        return (core, which, ep)

    def pair_copies():
        sources = (
            (own_meta.at[1 - core], meta.at[0, core]),
            (gain_in, gains.at[core]),
            (gate_in, gate.at[core]),
            (up_in, up.at[core]),
            (down_in, down.at[core]),
        )
        return [
            remote(src, dst, pair_send.at[n], pair_recv.at[n], sibling)
            for n, (src, dst) in enumerate(sources)
        ]

    def own_copies():
        sources = (
            (tokens.at[core], blocks.at[0, 0]),
            (named_in, named),
            (weight_in, weight),
            (gain_in, gains.at[core]),
            (gate_in, gate.at[core]),
            (up_in, up.at[core]),
            (down_in, down.at[core]),
        )
        return [
            pltpu.make_async_copy(src, dst, local_sem.at[n]) for n, (src, dst) in enumerate(sources)
        ]

    pair, own = pair_copies(), own_copies()
    for copy in own:
        copy.start()

    barrier = pltpu.get_barrier_semaphore()
    friends = [sibling, at_y(1), at_y(2), at_y(3), at_x(x_one), at_x(x_three)]
    if any(DIRECT):
        friends += [at_x(x_two)]
    friends += [at_z(step) for step in (-3, -2, -1, 1, 2, 3)]
    for friend in friends:
        pl.semaphore_signal(barrier, inc=1, device_id=friend, device_id_type=MESH)
    own[1].wait()
    own[2].wait()
    for micro in range(2):
        entry = jnp.concatenate([named[micro].astype(F32), weight[micro]], axis=0)
        own_meta[micro] = jnp.concatenate([entry, entry], axis=1).astype(BF)
    meta[0, core] = own_meta[core]
    own[0].wait()
    pl.semaphore_wait(barrier, len(friends))

    for copy in pair:
        copy.start()

    def gather(layer, distance, piece):
        parent, step = PARENT[distance]
        p = AT[distance]
        span = pl.ds(piece * PIECE, PIECE)
        return remote(
            blocks.at[layer, AT[parent], span],
            blocks.at[layer, p, span],
            zg_send.at[layer, p, piece],
            zg_recv.at[layer, p, piece],
            at_z(step),
        )

    def gather_meta(distance):
        parent, step = PARENT[distance]
        p = AT[distance]
        return remote(meta.at[AT[parent]], meta.at[p], zm_send.at[p], zm_recv.at[p], at_z(step))

    def reduce(layer, distance, piece):
        _, step = PARENT[distance]
        p = AT[distance]
        span = pl.ds(piece * PIECE, PIECE)
        return remote(
            ring_out.at[layer, p, span],
            ring_in.at[layer, p, span],
            zr_send.at[layer, p, piece],
            zr_recv.at[layer, p, piece],
            at_z(-step),
        )

    def y_go(layer, g, k):
        return remote(
            chosen.at[layer, g, pl.ds(k * PART, PART)],
            rows.at[layer, g, 0, pl.ds(k * PART, PART)],
            yg_send.at[layer, g, k],
            yg_recv.at[layer, g, k],
            at_y(TURN[k]),
        )

    def y_back(layer, g, k):
        return remote(
            done.at[layer, g, pl.ds(k * PART, PART)],
            back.at[layer, g, pl.ds(k * PART, PART)],
            yr_send.at[layer, g, k],
            yr_recv.at[layer, g, k],
            at_y(-TURN[k]),
        )

    def x_gather(layer, g, h):
        first, second = (1, 3) if h == 0 else (3, 1)
        span = pl.ds(h * HALF, HALF)
        source = 0 if DIRECT[g] else first
        far = 2 if DIRECT[g] else second
        return [
            remote(
                rows.at[layer, g, src, span],
                rows.at[layer, g, dst, span],
                xg_send.at[layer, g, h, n],
                xg_recv.at[layer, g, h, n],
                at_x(quarter[to]),
            )
            for n, (src, dst, to) in enumerate(
                ((0, first, first), (0, second, second), (source, 2, far))
            )
        ]

    def x_reduce(layer, g, h):
        first, second = (1, 3) if h == 0 else (3, 1)
        span = pl.ds(h * HALF, HALF)
        if DIRECT[g]:
            ways = [(parts.at[layer, g, n, span], n) for n in (2, 1, 3)]
        else:
            ways = [
                (parts.at[layer, g, 2, span], first),
                (parts.at[layer, g, first, span], first),
                (half_out.at[layer, g, span], second),
            ]
        return [
            remote(
                src,
                half.at[layer, g, n, span],
                xr_send.at[layer, g, h, n],
                xr_recv.at[layer, g, h, n],
                at_x(quarter[to]),
            )
            for n, (src, to) in enumerate(ways)
        ]

    def build_selection(layer, pairs):
        lane = lax.broadcasted_iota(jnp.int32, (2 * TOPK, 128), 1)
        low = lane < TOK
        a = lax.broadcasted_iota(jnp.int32, (128, 128), 0)
        b = lax.broadcasted_iota(jnp.int32, (128, 128), 1)
        before = jnp.where((a < b) & ((a < TOK) == (b < TOK)), 1.0, 0.0).astype(BF)
        row_number = lax.broadcasted_iota(jnp.int32, (PART, 128), 0).astype(F32)
        high_one = jnp.where(lax.broadcasted_iota(jnp.int32, (1, 128), 1) < TOK, 0.0, 1.0)
        for q in pairs:
            entry = jnp.where(
                low, meta[2 * q, layer].astype(F32), meta[2 * q + 1, layer].astype(F32)
            )
            named, weight = entry[:TOPK], entry[TOPK:]
            same = [
                jnp.where(named == (z * NY + (y + TURN[k]) % NY).astype(F32), 1.0, 0.0)
                for k in range(NY)
            ]
            count = jnp.dot(
                jnp.concatenate(same, axis=0).astype(BF), before, preferred_element_type=F32
            )
            for k in range(NY):
                position = jnp.sum(count[k * TOPK : (k + 1) * TOPK], axis=0, keepdims=True)
                hits = jnp.sum(same[k], axis=0, keepdims=True)
                share = jnp.sum(same[k] * weight, axis=0, keepdims=True)
                slot = jnp.where(hits > 0.5, position + CAP * (2 * q + high_one), -1.0)
                for m, (other, g) in enumerate(MIXES):
                    if other == q:
                        hit = row_number + g * PART == slot
                        at = (q - PAIRS[g][0]) * 128
                        pick[layer, g, k * PART : (k + 1) * PART, at : at + 128] = jnp.where(
                            hit, 1.0, 0.0
                        ).astype(BF)
                        mix[layer, m, k * PART : (k + 1) * PART, :] = jnp.where(
                            hit, share, 0.0
                        ).astype(BF)

    def expert(layer, g, h):
        span_rows = slice(h * HALF, (h + 1) * HALF)
        total = jnp.zeros((HALF, 1), F32)
        for s in range(4):
            value = rows[layer, g, s, span_rows].astype(F32)
            total = total + jnp.sum(value * value, axis=1, keepdims=True)
        scale = lax.rsqrt(total / D + EPSILON)
        gate_act = jnp.zeros((HALF, FFQ), F32)
        up_act = jnp.zeros((HALF, FFQ), F32)
        for s in range(4):
            span = pl.ds(pl.multiple_of(quarter[s] * Q, Q), Q)
            value = rows[layer, g, s, span_rows].astype(F32)
            normed = (value * scale * gains[layer, 0:1, span]).astype(BF)
            gate_act += jnp.dot(normed, gate[layer, span, :], preferred_element_type=F32)
            up_act += jnp.dot(normed, up[layer, span, :], preferred_element_type=F32)
        hidden = (gate_act / (1.0 + jnp.exp(-gate_act)) * up_act).astype(BF)
        sends = x_reduce(layer, g, h)
        first = 1 if h == 0 else 3
        order = (2, 1, 3, 0) if DIRECT[g] else (2, first, 4 - first, 0)
        for n, s in enumerate(order):
            span = pl.ds(pl.multiple_of(quarter[s] * Q, Q), Q)
            parts[layer, g, s, span_rows] = jnp.dot(
                hidden, down[layer, :, span], preferred_element_type=F32
            ).astype(BF)
            if n < (3 if DIRECT[g] else 2):
                sends[n].start()

    across = remote(results.at[1 - core], out.at[core], pair_send.at[5], pair_recv.at[5], sibling)
    keep = pltpu.make_async_copy(results.at[core], out.at[core], local_sem.at[0])

    def one_layer(layer, carry):
        sums = {}

        def first_only(action):
            pl.when(layer == 0)(action)

        def z_pass(*roots):
            if roots == (0,):
                for distance in CHILDREN[0]:
                    for piece in range(PIECES):
                        gather(layer, distance, piece).start()
            else:
                for piece in range(PIECES):
                    for root in roots:
                        gather(layer, root, piece).wait_recv()
                        for distance in CHILDREN[root]:
                            gather(layer, distance, piece).start()

            @first_only
            def _():
                for root in roots:
                    if root:
                        gather_meta(root).wait_recv()
                    else:
                        pair[0].wait()
                    for distance in CHILDREN[root]:
                        gather_meta(distance).start()

        def z_wait(*distances):
            for distance in distances:
                for piece in range(PIECES):
                    gather(layer, distance, piece).wait_recv()

            @first_only
            def _():
                for distance in distances:
                    gather_meta(distance).wait_recv()

        def build(*pairs):
            first_only(lambda: build_selection(0, pairs))

        def build_next():
            first_only(lambda: build_selection(1, range(NZ // 2)))

        def select(g):
            pairs = PAIRS[g]
            source = blocks[layer, 2 * pairs[0] : 2 * pairs[-1] + 2].reshape(-1, Q)
            value = jnp.dot(
                pick[layer, g, :, 0 : len(pairs) * 128], source, preferred_element_type=F32
            ).astype(BF)
            chosen[layer, g] = value
            for k in (1, 2, 3):
                y_go(layer, g, k).start()
            rows[layer, g, 0, 0:PART] = value[:PART]

        def x_send(g, h):
            for k in (2 * h, 2 * h + 1):
                if k:
                    y_go(layer, g, k).wait_recv()
            copies = x_gather(layer, g, h)
            for copy in copies if DIRECT[g] else copies[:2]:
                copy.start()

        def x_pass(g, h):
            copies = x_gather(layer, g, h)
            copies[0].wait_recv()
            if not DIRECT[g]:
                copies[2].start()

        def weights():
            @first_only
            def _():
                for copy in pair[1:] + own[3:]:
                    copy.wait()

        def work(g, h):
            copies = x_gather(layer, g, h)
            copies[1].wait_recv()
            copies[2].wait_recv()
            expert(layer, g, h)

        def fold(g, h):
            if not DIRECT[g]:
                span = slice(h * HALF, (h + 1) * HALF)
                copies = x_reduce(layer, g, h)
                copies[0].wait_recv()
                half_out[layer, g, span] = (
                    parts[layer, g, 3 - 2 * h, span].astype(F32)
                    + half[layer, g, 0, span].astype(F32)
                ).astype(BF)
                copies[2].start()

        def finish(g, h):
            span = slice(h * HALF, (h + 1) * HALF)
            copies = x_reduce(layer, g, h)
            terms = (0, 1, 2) if DIRECT[g] else (1, 2)
            for n in terms:
                copies[n].wait_recv()
            value = parts[layer, g, 0, span].astype(F32)
            for n in terms:
                value = value + half[layer, g, n, span].astype(F32)
            value = value.astype(BF)
            done[layer, g, span] = value
            for k in (2 * h, 2 * h + 1):
                if k:
                    y_back(layer, g, k).start()
            if h == 0:
                back[layer, g, 0:PART] = value[:PART]

        def returned(g):
            for k in (1, 2, 3):
                y_back(layer, g, k).wait_recv()

        def collect(distance, piece, value):
            for child in CHILDREN.get(distance, ()):
                reduce(layer, child, piece).wait_recv()
                span = slice(piece * PIECE, (piece + 1) * PIECE)
                value = value + ring_in[layer, AT[child], span].astype(F32)
            return value

        def pass_on(*distances):
            for piece in range(PIECES):
                span = slice(piece * PIECE, (piece + 1) * PIECE)
                for distance in distances:
                    value = collect(distance, piece, sums[distance][span])
                    ring_out[layer, AT[distance], span] = value.astype(BF)
                    reduce(layer, distance, piece).start()

        def combine(q):
            value = None
            for m, (other, g) in enumerate(MIXES):
                if other == q:
                    term = lax.dot_general(
                        mix[layer, m],
                        back[layer, g],
                        (((0,), (0,)), ((), ())),
                        preferred_element_type=F32,
                    )
                    value = term if value is None else value + term
            for k in range(2):
                distance = PLACE[2 * q + k]
                sums[distance] = value[k * TOK : (k + 1) * TOK]
                if distance not in CHILDREN:
                    pass_on(distance)

        def settle():
            for distance in PLACE[1:]:
                for piece in range(PIECES):
                    gather(layer, distance, piece).wait_send()
                    if distance not in (3, 13):
                        reduce(layer, distance, piece).wait_send()

            @first_only
            def _():
                for distance in PLACE[1:]:
                    gather_meta(distance).wait_send()

            for g in range(GROUPS):
                for k in (1, 2, 3):
                    y_go(layer, g, k).wait_send()
                    y_back(layer, g, k).wait_send()
                for h in range(2):
                    for copy in x_gather(layer, g, h) + x_reduce(layer, g, h):
                        copy.wait_send()

        def last():
            for piece in range(PIECES):
                span = slice(piece * PIECE, (piece + 1) * PIECE)
                value = sums[0][span] + blocks[layer, 0, span].astype(F32)
                final = collect(0, piece, value).astype(BF)
                results[layer, span] = final

                @first_only
                def _():
                    blocks[1, 0, span] = final

                for distance in (3, 13):
                    reduce(layer, distance, piece).wait_send()

            pl.when(layer == core)(keep.start)
            pl.when(layer != core)(across.start)

        steps = dict(
            z=z_pass, zw=z_wait, b=build, bn=build_next, s=select, xs=x_send, xp=x_pass,
            w=weights, e=work, f=fold, d=finish, r=returned, c=combine, p=pass_on,
            settle=settle, last=last,
        )
        def hold():
            @pl.when((layer == 0) & (core == 1))
            def _():
                pl.semaphore_wait(turn, 1)

        def hand_over():
            @pl.when((layer == 0) & (core == 0))
            def _():
                pl.semaphore_signal(turn, inc=1, device_id=sibling, device_id_type=MESH)

        steps["turn"] = hand_over
        steps["hold"] = hold
        for step in SCHEDULE:
            name, *places = step.split()
            steps[name](*[int(place) for place in places])
        return carry

    lax.fori_loop(0, 2, one_layer, 0)
    across.wait()
    keep.wait()


def shards(tokens, norm_gain, expert_gate, expert_up, expert_down, routes, route_weights):
    named = jnp.swapaxes(routes[0], 1, 2)
    weight = jnp.swapaxes(route_weights[0], 1, 2)
    anywhere = pl.BlockSpec(memory_space=pl.ANY)
    dma = pltpu.SemaphoreType.DMA
    out = pl.pallas_call(
        kernel,
        out_shape=jax.ShapeDtypeStruct((2, TOK, Q), BF),
        in_specs=[anywhere] * 7,
        out_specs=anywhere,
        scratch_shapes=[
            pltpu.VMEM((2, D, FFQ), BF),
            pltpu.VMEM((2, D, FFQ), BF),
            pltpu.VMEM((2, FFQ, D), BF),
            pltpu.VMEM((2, 1, D), F32),
            pltpu.VMEM((2, NZ, TOK, Q), BF),
            pltpu.VMEM((2, TOPK, TOK), jnp.int32),
            pltpu.VMEM((2, TOPK, TOK), F32),
            pltpu.VMEM((2, 2 * TOPK, 128), BF),
            pltpu.VMEM((NZ, 2, 2 * TOPK, 128), BF),
            pltpu.VMEM((2, GROUPS, WIDE, Q), BF),
            pltpu.VMEM((2, GROUPS, 4, WIDE, Q), BF),
            pltpu.VMEM((2, GROUPS, 4, WIDE, Q), BF),
            pltpu.VMEM((2, GROUPS, 3, WIDE, Q), BF),
            pltpu.VMEM((2, GROUPS, WIDE, Q), BF),
            pltpu.VMEM((2, GROUPS, WIDE, Q), BF),
            pltpu.VMEM((2, GROUPS, WIDE, Q), BF),
            pltpu.VMEM((2, GROUPS, WIDE, 512), BF),
            pltpu.VMEM((2, len(MIXES), WIDE, 128), BF),
            pltpu.VMEM((2, NZ, TOK, Q), BF),
            pltpu.VMEM((2, NZ, TOK, Q), BF),
            pltpu.VMEM((2, TOK, Q), BF),
            dma((7,)),
            dma((6,)),
            dma((6,)),
            dma((2, NZ, PIECES)),
            dma((2, NZ, PIECES)),
            dma((NZ,)),
            dma((NZ,)),
            dma((2, GROUPS, NY)),
            dma((2, GROUPS, NY)),
            dma((2, GROUPS, NY)),
            dma((2, GROUPS, NY)),
            dma((2, GROUPS, 2, 3)),
            dma((2, GROUPS, 2, 3)),
            dma((2, GROUPS, 2, 3)),
            dma((2, GROUPS, 2, 3)),
            dma((2, NZ, PIECES)),
            dma((2, NZ, PIECES)),
            pltpu.SemaphoreType.REGULAR,
        ],
        compiler_params=pltpu.CompilerParams(
            collective_id=0, has_side_effects=True, vmem_limit_bytes=56 * 1024 * 1024
        ),
        cost_estimate=pl.CostEstimate(
            flops=2 * 2 * 576 * D * 768, bytes_accessed=8 * 1024 * 1024, transcendentals=0
        ),
    )(tokens, norm_gain, named, weight, expert_gate[0, 0], expert_up[0, 0], expert_down[0, 0])
    return out[None]


def solution(mesh):
    placed = (
        P(None, "ep", "tp"),
        P("section", None),
        P("section", "ep", None, "tp"),
        P("section", "ep", None, "tp"),
        P("section", "ep", "tp", None),
        P("section", None, "ep", None),
        P("section", None, "ep", None),
    )
    return jax.shard_map(
        shards,
        mesh=mesh,
        in_specs=placed,
        out_specs=P("section", None, "ep", "tp"),
        check_vma=False,
    )
```
